512 devices in a mesh: row: 16 (over z), col: 32 (over x, y, core).
Axes of the slice: x: 4, y: 4, z: 16, core: 2. Of those that a mesh axis runs over, the one named last changes fastest.
Arguments:
- tokens: bfloat16 [2048, 7168], P(('row', 'col')), may hold values from -6 to 6
- gate_up: bfloat16 [32, 2, 1536, 7168], P('col', None, 'row'), may hold values from -0.0625 to 0.0625
- down: bfloat16 [32, 1536, 7168], P('col', None, 'row'), may hold values from -0.15625 to 0.15625
- expert_ids: int32 [2048, 8], replicated, may hold values from 0 to 31, all different within a row; in each aligned block of 128 rows (0 to 127, 128 to 255, ...) at most 48 rows name the same one
- gate_weights: float32 [2048, 8], replicated, may hold values from 0.05 to 1
- capacity: int32 [32], replicated, may hold values from 24 to 48
Outputs:
- routed_out: bfloat16 [2048, 7168], P(('row', 'col'))
The draws below stay inside these ranges and needn't reach their ends.
Inputs may be any that keep to these rules, and one draw needn't show every extreme that they name: `expert_ids`: each row names 8 different experts; within each aligned group of 128 rows no expert is named by more than 48 rows.
All inputs are finite; a program needn't handle non-finite values.
Results may differ from the reference program's by a relative error of at most 0.0063.
Values may be sent and summed in bfloat16 or wider, within the bound.
No kernel may reach another device: no remote copies, remote signals or barrier semaphores. Data moves between devices by JAX's collectives and lax.ppermute only.
A program may use at most 64 MiB of HBM per device.

```python
import math
import jax
import jax.numpy as jnp
import numpy as np
from jax import lax

D = 7168
TOP = 8
MOE_H = 1536
TOK_DEV = 4
EXPERTS = 32
TOKENS = 2048
RCAP = 48
N_ROW = 16
N_COL = 32


def draw_capacity(key, part):
    key = jax.random.fold_in(key, 7)
    value_key, pick_key = jax.random.split(key)
    values = jax.random.randint(value_key, (EXPERTS,), RCAP // 2, RCAP + 1)
    chosen = jax.random.randint(pick_key, (), 0, EXPERTS)
    return jnp.where(jnp.arange(EXPERTS) == chosen, RCAP, values).astype(jnp.int32)


def block_levels(own_key, shape, cuts, smallest, largest):
    level = 1.0
    for dim, shards_of in cuts:
        heights = jax.random.uniform(jax.random.fold_in(jax.random.fold_in(own_key, 6), dim), (shards_of,), jnp.float32, smallest / len(cuts), largest / len(cuts))
        level = level * jnp.repeat(jnp.exp(heights), shape[dim] // shards_of).reshape((-1,) + (1,) * (len(shape) - 1 - dim))
    return level


def deal_out(key, own, number, rows, number_of, top, most, lean):
    ranking = jax.random.permutation(key, number_of)
    packed, usual = load_shares(number_of, rows * top, most, lean, True), load_shares(number_of, rows * top, most, lean, False)
    places = jnp.arange(number_of)

    def named(sizes, rotation):
        used = int((sizes > 0).sum())
        fixed = max(1, used // 4)
        moved = fixed + (places - fixed + rotation * (used - fixed)) % max(1, number_of - fixed)
        return jnp.zeros((number_of,), jnp.int32).at[ranking[jnp.where(places < fixed, places, moved)]].set(jnp.asarray(sizes, jnp.int32))

    sizes = jnp.where(number % 4 == 0, named(packed, number // 4), named(usual, number - number // 4 - 1))
    mixed = jax.random.permutation(jax.random.fold_in(own, 3), number_of)
    source_of, taker = mixed[0:number_of // 2 * 2:2], mixed[1:number_of // 2 * 2:2]
    room = jnp.minimum(sizes[source_of] - 1, most - sizes[taker]) // 2
    room = jnp.where((source_of == ranking[0]) | (taker == ranking[0]) | (sizes[taker] == 0), 0, jnp.maximum(room, 0))
    moved = jax.random.randint(jax.random.fold_in(own, 4), (number_of // 2,), 0, 1 << 20) % (room + 1)
    sizes = sizes.at[source_of].add(-moved).at[taker].add(moved)
    items = jnp.searchsorted(jnp.cumsum(sizes), jnp.arange(rows * top), side="right").astype(jnp.int32)
    grid = items.reshape(top, rows).T
    grid = grid[jax.random.permutation(jax.random.fold_in(own, 1), rows)]
    rotation = jax.random.randint(jax.random.fold_in(own, 2), (rows, 1), 0, top)
    return jnp.take_along_axis(grid, (jnp.arange(top)[None, :] + rotation) % top, axis=1)


def load_shares(number_of, total, most, lean, full):
    weights = [(1 << 20) // math.isqrt(grade ** lean) + 1 for grade in range(1, number_of + 1)]
    largest = most if full else min(most, max(-(-total // number_of), total * weights[0] // sum(weights)))
    least = 1 if total - largest >= number_of - 1 else 0
    given, spare = [largest] + [least] * (number_of - 1), total - largest - least * (number_of - 1)
    while spare > 0:
        candidates = [i for i in range(1, number_of) if given[i] < largest] or [i for i in range(1, number_of) if given[i] < most]
        whole, budget = sum([weights[i] for i in candidates]), spare
        for i in candidates:
            more = min(most - given[i], max(1, budget * weights[i] // whole), spare)
            given[i] = given[i] + more
            spare = spare - more
    return np.array(given)


def gaussian(own_key, dims, deviation, limit, shards=(), kind=jnp.bfloat16):
    array = deviation * jax.random.normal(own_key, dims, jnp.float32)
    if shards:
        array = array * block_levels(own_key, dims, shards, -0.22, 0.18)
    return jnp.clip(array, -limit, limit).astype(kind)


def setup_inputs(seed: int = 0) -> dict:
    arg_keys = jax.random.split(jax.random.key(seed), 7)
    tokens = gaussian(arg_keys[0], (TOKENS, D), 1.0, 6.0, ((0, 512),))
    gate_up = gaussian(arg_keys[1], (EXPERTS, 2, MOE_H, D), D ** -0.5, 0.0625, ((0, 32), (2, 16)))
    down = gaussian(arg_keys[2], (EXPERTS, MOE_H, D), MOE_H ** -0.5, 0.15625, ((0, 32), (2, 16)))
    expert_ids_keys = jax.random.split(jax.random.fold_in(arg_keys[3], 1), TOKENS // (N_COL * TOK_DEV))
    expert_ids_turns = jax.random.permutation(jax.random.fold_in(arg_keys[3], 3), TOKENS // (N_COL * TOK_DEV))
    expert_ids = jax.vmap(lambda own, number: deal_out(jax.random.fold_in(arg_keys[3], 2), own, number, N_COL * TOK_DEV, EXPERTS, TOP, RCAP, 2))(expert_ids_keys, expert_ids_turns).reshape((TOKENS, TOP))
    gate_weights = jnp.clip(jnp.exp(jax.random.uniform(arg_keys[4], (TOKENS, TOP), jnp.float32, math.log(0.05), math.log(1.0))), 0.05, 1.0)
    capacity = draw_capacity(jax.random.fold_in(arg_keys[6], 71), 0)
    return {"tokens": tokens, "gate_up": gate_up, "down": down, "expert_ids": expert_ids, "gate_weights": gate_weights, "capacity": capacity}


def expert_slots(expert_ids, gate_weights, capacity, expert):
    total_rows = expert_ids.shape[0]
    block_rows = N_COL * TOK_DEV
    member = expert_ids == expert
    hit_count = jnp.sum(member.astype(jnp.int32), axis=1).astype(jnp.int32)
    grouped = hit_count.reshape(total_rows // block_rows, block_rows)
    rank_in = (jnp.cumsum(grouped, axis=1).astype(jnp.int32) - grouped).reshape(total_rows)
    cap_here = lax.dynamic_index_in_dim(capacity, expert, 0, keepdims=False)
    usable = (hit_count > 0) & (rank_in < cap_here)
    weights = jnp.sum(jnp.where(member, gate_weights, 0.0), axis=1)
    groups = jnp.arange(total_rows, dtype=jnp.int32) // block_rows
    slot_ids = jnp.where(usable, groups * RCAP + rank_in, -1).astype(jnp.int32)
    return slot_ids, weights


def reference(tokens, gate_up, down, expert_ids, gate_weights, capacity):
    slot_count = N_ROW * RCAP
    slot_index = jnp.arange(slot_count, dtype=jnp.int32)

    def one_expert(running, inputs):
        weights_gu, weights_down, expert = inputs
        slot_ids, weights = expert_slots(expert_ids, gate_weights, capacity, expert)
        select = (slot_index[:, None] == slot_ids[None, :]).astype(jnp.bfloat16)
        picked = jnp.dot(select, tokens, preferred_element_type=jnp.float32).astype(jnp.bfloat16)
        gate_part = jnp.dot(picked, weights_gu[0].T, preferred_element_type=jnp.float32)
        up_part = jnp.dot(picked, weights_gu[1].T, preferred_element_type=jnp.float32)
        hidden = (jax.nn.silu(gate_part) * up_part).astype(jnp.bfloat16)
        outputs = jnp.dot(hidden, weights_down, preferred_element_type=jnp.float32).astype(jnp.bfloat16)
        combine = jnp.where(slot_ids[:, None] == slot_index[None, :], weights[:, None], 0.0).astype(jnp.bfloat16)
        return running + jnp.dot(combine, outputs, preferred_element_type=jnp.float32), None

    initial = jnp.zeros(tokens.shape, jnp.float32)
    summed, unused = lax.scan(one_expert, initial, (gate_up, down, jnp.arange(EXPERTS, dtype=jnp.int32)))
    return summed.astype(jnp.bfloat16)
```

```python
import jax
import jax.numpy as jnp
from jax import lax
from jax.sharding import Mesh, PartitionSpec as P

PARTS = (6, 5, 5)
SLOTS = 48
PLANE = ("x", "y")
PAIR = [(0, 1), (1, 0)]


def routing(expert_ids, gate_weights, capacity, expert, groups, group_rows):
    member = expert_ids == expert
    hits = jnp.sum(member.astype(jnp.int32), axis=1).reshape(groups, group_rows)
    rank = jnp.cumsum(hits, axis=1) - hits
    cap = lax.dynamic_index_in_dim(capacity, expert, 0, keepdims=False)
    weights = jnp.sum(jnp.where(member, gate_weights, 0.0), axis=1)
    slots = jnp.where((hits > 0) & (rank < cap), rank, -1)
    return slots, weights.reshape(groups, group_rows)


def local(tokens, gate_up, down, expert_ids, gate_weights, capacity):
    core = lax.axis_index("c")
    plane_index = lax.axis_index(PLANE)
    chips = lax.axis_size("x") * lax.axis_size("y")
    groups = lax.axis_size("z")
    own, width = tokens.shape
    half = width // 2
    pair = 2 * own
    group_rows = chips * pair
    mine, other = core * half, (1 - core) * half

    def half_of(array, start):
        return lax.dynamic_slice_in_dim(array, start, half, axis=array.ndim - 1)

    kept = half_of(tokens, mine)
    got = lax.ppermute(half_of(tokens, other), "c", PAIR)
    first = core == 0
    pair_tokens = jnp.concatenate(
        [jnp.where(first, kept, got), jnp.where(first, got, kept)], axis=0
    )
    line = lax.all_gather(pair_tokens, "z", axis=0, tiled=False)

    units = 2 * gate_up.shape[2]
    weights_all = gate_up[0].reshape(units, width)
    w_mine = half_of(weights_all, mine)
    w_other = lax.ppermute(half_of(weights_all, other), "c", PAIR)
    w_down = down[0]

    slots, route = routing(
        expert_ids, gate_weights, capacity, plane_index * 2 + core, groups, group_rows
    )

    gathered = []
    start = 0
    for count in PARTS:
        piece = line[start : start + count].reshape(count * pair, half)
        gathered.append(lax.all_gather(piece, PLANE, axis=0, tiled=True))
        start += count

    rows_out = []
    start = 0
    contract = (((1,), (1,)), ((), ()))
    for count, part in zip(PARTS, gathered):
        ours = lax.dot_general(part, w_mine, contract, preferred_element_type=jnp.float32)
        theirs = lax.dot_general(part, w_other, contract, preferred_element_type=jnp.float32)
        both = ours + lax.ppermute(theirs, "c", PAIR)
        hidden = (jax.nn.silu(both[:, : units // 2]) * both[:, units // 2 :]).astype(jnp.bfloat16)
        rows = count * group_rows
        n_slots = count * SLOTS
        offset = jnp.arange(count, dtype=jnp.int32)[:, None] * SLOTS
        slot_of = slots[start : start + count]
        slot_of = jnp.where(slot_of >= 0, slot_of + offset, -1).reshape(count, chips, pair)
        route_of = route[start : start + count].reshape(count, chips, pair)
        by_row = slot_of.transpose(1, 0, 2).reshape(rows)
        slot_index = jnp.arange(n_slots, dtype=jnp.int32)
        select = (by_row[:, None] == slot_index[None, :]).astype(jnp.bfloat16)
        picked = lax.dot_general(
            hidden, select, (((0,), (0,)), ((), ())), preferred_element_type=jnp.float32
        ).astype(jnp.bfloat16)
        all_hidden = lax.all_gather(picked, "z", axis=0, tiled=True)
        outputs = lax.dot_general(
            all_hidden, w_down, (((0,), (0,)), ((), ())), preferred_element_type=jnp.float32
        ).astype(jnp.bfloat16)

        def by_target(values):
            return values.reshape(count, chips, 2, own).transpose(2, 1, 0, 3).reshape(rows)

        to_slot, to_weight = by_target(slot_of), by_target(route_of)
        combine = jnp.where(
            to_slot[:, None] == slot_index[None, :], to_weight[:, None], 0.0
        ).astype(jnp.bfloat16)
        summed = jnp.dot(combine, outputs, preferred_element_type=jnp.float32)
        summed = summed.reshape(2, rows // 2, summed.shape[1])
        keep = lax.dynamic_index_in_dim(summed, core, 0, keepdims=False)
        give = lax.dynamic_index_in_dim(summed, 1 - core, 0, keepdims=False)
        chip_sum = (keep + lax.ppermute(give, "c", PAIR)).astype(jnp.bfloat16)
        arrived = lax.all_to_all(chip_sum, PLANE, split_axis=0, concat_axis=0, tiled=True)
        arrived = arrived.reshape(chips, count, own, arrived.shape[1]).astype(jnp.float32)
        rows_out.append(jnp.sum(arrived, axis=0).astype(jnp.bfloat16))
        start += count

    own_rows = jnp.concatenate(rows_out, axis=0)
    own_rows = lax.all_to_all(own_rows, "z", split_axis=0, concat_axis=0, tiled=True)
    return own_rows.transpose(1, 0, 2).reshape(own, width)


def solution(mesh):
    rows, cols = mesh.devices.shape
    side = 4
    fine = Mesh(mesh.devices.reshape(rows, side, cols // (2 * side), 2), ("z", "x", "y", "c"))
    col = ("x", "y", "c")
    in_specs = (
        P(("z",) + col, None),
        P(col, None, "z", None),
        P(col, None, "z"),
        P(),
        P(),
        P(),
    )
    out_specs = P(("z",) + col, None)
    return jax.shard_map(local, mesh=fine, in_specs=in_specs, out_specs=out_specs, check_vma=False)
```

```python
import jax
import jax.numpy as jnp
from jax import lax
from jax.sharding import Mesh, PartitionSpec as P

SLOTS = 48
LINE = ("zh", "zl")
PLANE = ("x", "y")
PAIR = [(0, 1), (1, 0)]


def routing(expert_ids, gate_weights, capacity, expert, groups, group_rows):
    member = expert_ids == expert
    hits = jnp.sum(member.astype(jnp.int32), axis=1).reshape(groups, group_rows)
    rank = jnp.cumsum(hits, axis=1) - hits
    cap = lax.dynamic_index_in_dim(capacity, expert, 0, keepdims=False)
    weights = jnp.sum(jnp.where(member, gate_weights, 0.0), axis=1)
    slots = jnp.where((hits > 0) & (rank < cap), rank, -1)
    return slots, weights.reshape(groups, group_rows)


def gather_near(block, near):
    size = lax.axis_size(near)
    from_left, from_right = [], []
    left, right = block, block
    for step in range(1, size):
        left = lax.ppermute(left, near, [(i, i + 1) for i in range(step - 1, size - 1)])
        right = lax.ppermute(right, near, [(i + 1, i) for i in range(0, size - step)])
        from_left.append(left)
        from_right.append(right)
    around = jnp.stack(from_left[::-1] + [block] + from_right)
    return lax.dynamic_slice_in_dim(around, size - 1 - lax.axis_index(near), size, axis=0)


def local(tokens, gate_up, down, expert_ids, gate_weights, capacity):
    core = lax.axis_index("c")
    plane_index = lax.axis_index(PLANE)
    near = lax.axis_index("zl")
    chips = lax.axis_size("x") * lax.axis_size("y")
    far_size, near_size = lax.axis_size("zh"), lax.axis_size("zl")
    groups = far_size * near_size
    own, width = tokens.shape
    half = width // 2
    pair = 2 * own
    group_rows = chips * pair
    class_rows = far_size * group_rows
    class_slots = far_size * SLOTS
    mine, other = core * half, (1 - core) * half

    def half_of(array, start):
        return lax.dynamic_slice_in_dim(array, start, half, axis=array.ndim - 1)

    kept = half_of(tokens, mine)
    got = lax.ppermute(half_of(tokens, other), "c", PAIR)
    first = core == 0
    pair_tokens = jnp.concatenate(
        [jnp.where(first, kept, got), jnp.where(first, got, kept)], axis=0
    )
    line = lax.all_gather(pair_tokens, LINE, axis=0, tiled=True)
    every = lax.all_gather(line, PLANE, axis=0, tiled=True)

    units = 2 * gate_up.shape[2]
    weights_all = gate_up[0].reshape(units, width)
    w_both = jnp.concatenate(
        [half_of(weights_all, mine), lax.ppermute(half_of(weights_all, other), "c", PAIR)], axis=0
    )
    w_down = gather_near(down[0], "zl")

    slots, route = routing(
        expert_ids, gate_weights, capacity, plane_index * 2 + core, groups, group_rows
    )

    both = lax.dot_general(
        every, w_both, (((1,), (1,)), ((), ())), preferred_element_type=jnp.float32
    )
    both = both[:, :units] + lax.ppermute(both[:, units:], "c", PAIR)
    hidden = (jax.nn.silu(both[:, : units // 2]) * both[:, units // 2 :]).astype(jnp.bfloat16)

    offset = jnp.arange(far_size, dtype=jnp.int32)[:, None, None] * SLOTS
    slots = slots.reshape(far_size, near_size, group_rows)
    slots = jnp.where(slots >= 0, slots + offset, -1)
    slot_index = jnp.arange(class_slots, dtype=jnp.int32)
    by_row = slots.reshape(far_size, near_size, chips, pair).transpose(1, 2, 0, 3)
    by_row = by_row.reshape(near_size, class_rows)
    select = (by_row[:, :, None] == slot_index).astype(jnp.bfloat16)
    hidden = hidden.reshape(chips, far_size, near_size, pair, units // 2)
    hidden = hidden.transpose(2, 0, 1, 3, 4).reshape(near_size, class_rows, units // 2)
    picked = lax.dot_general(
        hidden, select, (((1,), (1,)), ((0,), (0,))), preferred_element_type=jnp.float32
    ).astype(jnp.bfloat16)
    to_all = jnp.broadcast_to(picked, (far_size,) + picked.shape)
    to_all = to_all.reshape(groups * picked.shape[1], class_slots)
    all_hidden = lax.all_to_all(to_all, LINE, split_axis=0, concat_axis=0, tiled=True)
    outputs = jnp.concatenate(
        [
            lax.dot_general(
                all_hidden, w_down[i], (((0,), (0,)), ((), ())), preferred_element_type=jnp.float32
            ).astype(jnp.bfloat16)
            for i in range(near_size)
        ],
        axis=1,
    )

    def by_target(values):
        mine = lax.dynamic_index_in_dim(values, near, 1, keepdims=False)
        mine = mine.reshape(far_size, chips, 2, own).transpose(2, 1, 0, 3)
        return mine.reshape(class_rows)

    to_slot = by_target(slots)
    to_weight = by_target(route.reshape(slots.shape))
    combine = jnp.where(
        to_slot[:, None] == slot_index[None, :], to_weight[:, None], 0.0
    ).astype(jnp.bfloat16)
    combine = combine.reshape(2, class_rows // 2, class_slots)
    give = jnp.dot(
        lax.dynamic_index_in_dim(combine, 1 - core, 0, keepdims=False),
        outputs,
        preferred_element_type=jnp.float32,
    ).astype(jnp.bfloat16)
    got = lax.ppermute(give, "c", PAIR)
    keep = jnp.dot(
        lax.dynamic_index_in_dim(combine, core, 0, keepdims=False),
        outputs,
        preferred_element_type=jnp.float32,
    )
    chip_sum = (keep + got).astype(jnp.bfloat16)
    arrived = lax.all_to_all(chip_sum, PLANE, split_axis=0, concat_axis=0, tiled=True)
    arrived = arrived.reshape(chips, far_size * own, arrived.shape[1]).astype(jnp.float32)
    own_rows = jnp.sum(arrived, axis=0).astype(jnp.bfloat16)
    own_rows = lax.all_to_all(own_rows, "zh", split_axis=0, concat_axis=0, tiled=True)
    own_rows = own_rows.reshape(far_size, own, own_rows.shape[1])
    return own_rows.transpose(1, 0, 2).reshape(own, width)


def solution(mesh):
    rows, cols = mesh.devices.shape
    near, side = 4, 4
    shape = (rows // near, near, side, cols // (2 * side), 2)
    fine = Mesh(mesh.devices.reshape(shape), ("zh", "zl", "x", "y", "c"))
    row, col = LINE, PLANE + ("c",)
    in_specs = (
        P(row + col, None),
        P(col, None, row, None),
        P(col, None, row),
        P(),
        P(),
        P(),
    )
    out_specs = P(row + col, None)
    return jax.shard_map(local, mesh=fine, in_specs=in_specs, out_specs=out_specs, check_vma=False)
```

```python
import jax
import jax.numpy as jnp
from jax import lax
from jax.sharding import Mesh, PartitionSpec as P

SLOTS = 48
LINE = ("zh", "k", "p")
PLANE = ("x", "y")
PAIR = [(0, 1), (1, 0)]


def routing(expert_ids, gate_weights, capacity, expert):
    member = expert_ids == expert
    hits = jnp.sum(member.astype(jnp.int32), axis=2)
    rank = jnp.cumsum(hits, axis=1) - hits
    cap = lax.dynamic_index_in_dim(capacity, expert, 0, keepdims=False)
    weights = jnp.sum(jnp.where(member, gate_weights, 0.0), axis=2)
    offset = jnp.arange(hits.shape[0], dtype=jnp.int32)[:, None] * SLOTS
    return jnp.where((hits > 0) & (rank < cap), rank + offset, -1), weights


def local(tokens, gate_up, down, expert_ids, gate_weights, capacity):
    core = lax.axis_index("c")
    k, p = lax.axis_index("k"), lax.axis_index("p")
    plane_index = lax.axis_index(PLANE)
    chips = lax.axis_size("x") * lax.axis_size("y")
    far = lax.axis_size("zh")
    own, width = tokens.shape
    group_rows = chips * 2 * own
    class_rows = far * group_rows
    class_slots = far * SLOTS

    def of_class(values, which):
        values = values.reshape((far, 2, 2) + values.shape[1:])
        return lax.dynamic_index_in_dim(
            lax.dynamic_index_in_dim(values, p, 2, keepdims=False), which, 1, keepdims=False
        )

    line = lax.all_gather(tokens, LINE, axis=0, tiled=False)
    mine = of_class(line, core)
    got = lax.ppermute(of_class(line, 1 - core), "c", PAIR)
    first = core == 0
    chip_rows = jnp.stack([jnp.where(first, mine, got), jnp.where(first, got, mine)])
    chip_rows = chip_rows.reshape(2 * far * own, width)
    every = lax.all_gather(chip_rows, PLANE, axis=0, tiled=True)

    units = gate_up.shape[2]
    w_own = gate_up[0].reshape(2 * units, width)
    w_pair = lax.ppermute(w_own, "p", PAIR)
    d_own = down[0]
    d_pair = lax.ppermute(d_own, "p", PAIR)
    w_all = jnp.concatenate(
        [w_own, lax.ppermute(w_own, "c", PAIR), w_pair, lax.ppermute(w_pair, "c", PAIR)], axis=0
    )
    d_all = [[d_own, d_pair], [lax.ppermute(d_own, "c", PAIR), lax.ppermute(d_pair, "c", PAIR)]]

    ids = of_class(expert_ids.reshape(far * 4, group_rows, -1), core)
    gates = of_class(gate_weights.reshape(far * 4, group_rows, -1), core)

    def by_row(values):
        values = values.reshape(far, chips, 2, own).transpose(1, 2, 0, 3)
        return values.reshape(class_rows)

    slot_index = jnp.arange(class_slots, dtype=jnp.int32)
    hits, combine = [], []
    for expert in (plane_index * 2 + core, plane_index * 2 + 1 - core):
        slots, weights = routing(ids, gates, capacity, expert)
        hit = by_row(slots)[:, None] == slot_index[None, :]
        hits.append(hit.astype(jnp.bfloat16))
        combine.append(jnp.where(hit, by_row(weights)[:, None], 0.0).astype(jnp.bfloat16))
    combine = jnp.concatenate(combine, axis=1)

    both = lax.dot_general(
        w_all, every, (((1,), (1,)), ((), ())), preferred_element_type=jnp.float32
    )
    both = both.reshape(2, 2, 2, units, class_rows)
    hidden = (jax.nn.silu(both[:, :, 0]) * both[:, :, 1]).astype(jnp.bfloat16)

    outputs = []
    for e in range(2):
        picked = lax.dot_general(
            hidden[:, e].reshape(2 * units, class_rows),
            hits[e],
            (((1,), (0,)), ((), ())),
            preferred_element_type=jnp.float32,
        ).astype(jnp.bfloat16)
        picked = picked.reshape(2, units, class_slots)
        picked = jnp.where(p == 0, picked, picked[::-1]).reshape(2 * units, class_slots)
        all_hidden = lax.all_gather(picked, ("zh", "k"), axis=0, tiled=True)
        outputs.append(
            jnp.concatenate(
                [
                    lax.dot_general(
                        all_hidden, d, (((0,), (0,)), ((), ())), preferred_element_type=jnp.float32
                    ).astype(jnp.bfloat16)
                    for d in d_all[e]
                ],
                axis=1,
            )
        )
    outputs = jnp.concatenate(outputs, axis=0)

    summed = jnp.dot(combine, outputs, preferred_element_type=jnp.float32).astype(jnp.bfloat16)
    arrived = lax.all_to_all(summed, PLANE, split_axis=0, concat_axis=0, tiled=True)
    arrived = arrived.reshape(chips, 2 * far * own, arrived.shape[1]).astype(jnp.float32)
    rows = jnp.sum(arrived, axis=0).astype(jnp.bfloat16)
    features = rows.shape[1]

    rows = rows.reshape(2, far, own, features).transpose(1, 0, 2, 3)[:, None]
    here = (jnp.arange(2) == core)[None, :, None, None, None]
    send = jnp.where(here, rows, jnp.zeros((), rows.dtype)).reshape(far * 4 * own, features)
    recv = lax.all_to_all(send, ("zh", "k", "c"), split_axis=0, concat_axis=0, tiled=True)
    recv = recv.reshape(far, 2, 2, own, features)
    recv = lax.dynamic_index_in_dim(recv, k, 2, keepdims=False)
    recv = recv.reshape(far, 2, own, 2, features // 2)
    recv = jnp.where(p == 0, recv, recv[:, :, :, ::-1])
    return recv.transpose(2, 0, 1, 3, 4).reshape(own, width)


def solution(mesh):
    rows, cols = mesh.devices.shape
    side = 4
    shape = (rows // 4, 2, 2, side, cols // (2 * side), 2)
    fine = Mesh(mesh.devices.reshape(shape), LINE + PLANE + ("c",))
    row, col = LINE, PLANE + ("c",)
    in_specs = (
        P(row + col, None),
        P(col, None, row, None),
        P(col, None, row),
        P(),
        P(),
        P(),
    )
    out_specs = P(row + col, None)
    return jax.shard_map(local, mesh=fine, in_specs=in_specs, out_specs=out_specs, check_vma=False)
```

```python
import jax
import jax.numpy as jnp
from jax import lax
from jax.sharding import Mesh, PartitionSpec as P

SLOTS = 48
LINE = ("zh", "k", "p")
PLANE = ("x", "y")
CHIP = PLANE + ("c",)
PAIR = [(0, 1), (1, 0)]


def turned(block, phase, shift):
    nx, ny = lax.axis_size("x"), lax.axis_size("y")
    perm = []
    for x in range(nx):
        for y in range(ny):
            for c in range(2):
                along_x = c == phase
                to_x = (x + shift) % nx if along_x else x
                to_y = y if along_x else (y + shift) % ny
                perm.append(((x * ny + y) * 2 + c, (to_x * ny + to_y) * 2 + c))
    return lax.ppermute(block, CHIP, perm)


def ring(block, phase, other=None):
    half = block.shape[0] // 2
    behind = turned(block, phase, 1)
    ahead = turned(block, phase, -1)
    if other is not None:
        other, ahead, behind = lax.optimization_barrier((other, ahead, behind))
    far_low = turned(behind[:half], phase, 1)
    far_high = turned(ahead[half:], phase, -1)
    return (block, ahead, jnp.concatenate([far_low, far_high], axis=0), behind), other


def routing(expert_ids, gate_weights, capacity, expert):
    member = expert_ids == expert
    hits = jnp.sum(member.astype(jnp.int32), axis=2)
    rank = jnp.cumsum(hits, axis=1) - hits
    cap = lax.dynamic_index_in_dim(capacity, expert, 0, keepdims=False)
    weights = jnp.sum(jnp.where(member, gate_weights, 0.0), axis=2)
    offset = jnp.arange(hits.shape[0], dtype=jnp.int32)[:, None] * SLOTS
    return jnp.where((hits > 0) & (rank < cap), rank + offset, -1), weights


def local(tokens, gate_up, down, expert_ids, gate_weights, capacity):
    core = lax.axis_index("c")
    k, p = lax.axis_index("k"), lax.axis_index("p")
    plane_index = lax.axis_index(PLANE)
    chips = lax.axis_size("x") * lax.axis_size("y")
    far = lax.axis_size("zh")
    own, width = tokens.shape
    group_rows = chips * 2 * own
    class_rows = far * group_rows
    class_slots = far * SLOTS

    def of_class(values, which):
        values = values.reshape((far, 2, 2) + values.shape[1:])
        return lax.dynamic_index_in_dim(
            lax.dynamic_index_in_dim(values, p, 2, keepdims=False), which, 1, keepdims=False
        )

    line = lax.all_gather(tokens, LINE, axis=0, tiled=False)
    mine = of_class(line, core)
    got = lax.ppermute(of_class(line, 1 - core), "c", PAIR)
    first = core == 0
    chip_rows = jnp.stack([jnp.where(first, mine, got), jnp.where(first, got, mine)])
    chip_rows = chip_rows.reshape(2 * far * own, width)
    w_mine = lax.all_gather(gate_up[0], "p", axis=0, tiled=False)
    d_mine = lax.all_gather(down[0], "p", axis=0, tiled=False)
    units = gate_up.shape[2]
    w_mine = w_mine.reshape(4 * units, width)

    around, unused = ring(chip_rows, 0)
    row = jnp.concatenate(around, axis=0)
    parts, w_late = ring(row, 1, w_mine)
    w_theirs = lax.ppermute(w_late, "c", PAIR)

    ids = of_class(expert_ids.reshape(far * 4, group_rows, -1), core)
    gates = of_class(gate_weights.reshape(far * 4, group_rows, -1), core)

    def by_row(values):
        values = values.reshape(far, chips, 2, own).transpose(1, 2, 0, 3)
        return values.reshape(class_rows)

    def by_arrival(values):
        values = values.reshape(far, lax.axis_size("x"), lax.axis_size("y"), 2, own)
        values = jnp.roll(values, -lax.axis_index("x"), axis=1)
        values = jnp.roll(values, -lax.axis_index("y"), axis=2)
        x_first = values.transpose(2, 1, 3, 0, 4)
        y_first = values.transpose(1, 2, 3, 0, 4)
        return jnp.where(first, x_first, y_first).reshape(class_rows)

    slot_index = jnp.arange(class_slots, dtype=jnp.int32)
    hits, combine = [], []
    for expert in (plane_index * 2 + core, plane_index * 2 + 1 - core):
        slots, weights = routing(ids, gates, capacity, expert)
        hits.append((by_arrival(slots)[:, None] == slot_index[None, :]).astype(jnp.bfloat16))
        target = by_row(slots)[:, None] == slot_index[None, :]
        combine.append(jnp.where(target, by_row(weights)[:, None], 0.0).astype(jnp.bfloat16))
    combine = jnp.concatenate(combine, axis=1)

    contract = (((1,), (1,)), ((), ()))
    both = [
        jnp.concatenate(
            [lax.dot_general(w, t, contract, preferred_element_type=jnp.float32) for t in parts],
            axis=1,
        ).reshape(2, 2, units, class_rows)
        for w in (w_mine, w_theirs)
    ]
    hidden = [(jax.nn.silu(b[:, 0]) * b[:, 1]).astype(jnp.bfloat16) for b in both]
    d_late, hidden = lax.optimization_barrier((d_mine, hidden))
    d_theirs = lax.ppermute(d_late, "c", PAIR)

    outputs = []
    for e in range(2):
        picked = lax.dot_general(
            hidden[e].reshape(2 * units, class_rows),
            hits[e],
            (((1,), (0,)), ((), ())),
            preferred_element_type=jnp.float32,
        ).astype(jnp.bfloat16)
        all_hidden = lax.all_gather(picked, ("zh", "k"), axis=0, tiled=True)
        outputs.append(
            jnp.concatenate(
                [
                    lax.dot_general(
                        all_hidden, d, (((0,), (0,)), ((), ())), preferred_element_type=jnp.float32
                    ).astype(jnp.bfloat16)
                    for d in (d_mine, d_theirs)[e]
                ],
                axis=1,
            )
        )
    outputs = jnp.concatenate(outputs, axis=0)

    summed = jnp.dot(combine, outputs, preferred_element_type=jnp.float32).astype(jnp.bfloat16)
    arrived = lax.all_to_all(summed, PLANE, split_axis=0, concat_axis=0, tiled=True)
    arrived = arrived.reshape(chips, 2 * far * own, arrived.shape[1]).astype(jnp.float32)
    rows = jnp.sum(arrived, axis=0).astype(jnp.bfloat16)
    features = rows.shape[1]

    rows = rows.reshape(2, far, own, features).transpose(1, 0, 2, 3)[:, None]
    here = (jnp.arange(2) == core)[None, :, None, None, None]
    send = jnp.where(here, rows, jnp.zeros((), rows.dtype)).reshape(far * 4 * own, features)
    recv = lax.all_to_all(send, ("zh", "k", "c"), split_axis=0, concat_axis=0, tiled=True)
    recv = recv.reshape(far, 2, 2, own, features)
    recv = lax.dynamic_index_in_dim(recv, k, 2, keepdims=False)
    return recv.transpose(2, 0, 1, 3).reshape(own, width)


def solution(mesh):
    rows, cols = mesh.devices.shape
    side = 4
    shape = (rows // 4, 2, 2, side, cols // (2 * side), 2)
    fine = Mesh(mesh.devices.reshape(shape), LINE + PLANE + ("c",))
    row, col = LINE, PLANE + ("c",)
    in_specs = (
        P(row + col, None),
        P(col, None, row, None),
        P(col, None, row),
        P(),
        P(),
        P(),
    )
    out_specs = P(row + col, None)
    return jax.shard_map(local, mesh=fine, in_specs=in_specs, out_specs=out_specs, check_vma=False)
```

```python
import jax
import jax.numpy as jnp
from jax import lax
from jax.sharding import Mesh, PartitionSpec as P

SLOTS = 48
LINE = ("zh", "k", "p")
PLANE = ("x", "y")
PAIR = [(0, 1), (1, 0)]


def routing(expert_ids, gate_weights, capacity, expert):
    member = expert_ids == expert
    hits = jnp.sum(member.astype(jnp.int32), axis=2)
    rank = jnp.cumsum(hits, axis=1) - hits
    cap = lax.dynamic_index_in_dim(capacity, expert, 0, keepdims=False)
    weights = jnp.sum(jnp.where(member, gate_weights, 0.0), axis=2)
    offset = jnp.arange(hits.shape[0], dtype=jnp.int32)[:, None] * SLOTS
    return jnp.where((hits > 0) & (rank < cap), rank + offset, -1), weights


def local(tokens, gate_up, down, expert_ids, gate_weights, capacity):
    core = lax.axis_index("c")
    k, p = lax.axis_index("k"), lax.axis_index("p")
    plane_index = lax.axis_index(PLANE)
    chips = lax.axis_size("x") * lax.axis_size("y")
    far = lax.axis_size("zh")
    own, width = tokens.shape
    group_rows = chips * 2 * own
    class_rows = far * group_rows
    class_slots = far * SLOTS

    def of_class(values, which):
        values = values.reshape((far, 2, 2) + values.shape[1:])
        return lax.dynamic_index_in_dim(
            lax.dynamic_index_in_dim(values, p, 2, keepdims=False), which, 1, keepdims=False
        )

    units = gate_up.shape[2]
    w_own = gate_up[0].reshape(2 * units, width)
    gate_pair = lax.ppermute(w_own[:units], "p", PAIR)
    line = lax.all_gather(tokens, LINE, axis=0, tiled=False)
    line, gate_pair = lax.optimization_barrier((line, gate_pair))
    mine = of_class(line, core)
    got = lax.ppermute(of_class(line, 1 - core), "c", PAIR)
    first = core == 0
    up_pair = lax.ppermute(w_own[units:], "p", PAIR)

    chip_rows = jnp.stack([jnp.where(first, mine, got), jnp.where(first, got, mine)])
    chip_rows = chip_rows.reshape(2 * far * own, width)
    every = lax.all_gather(chip_rows, PLANE, axis=0, tiled=True)

    w_all = lax.optimization_barrier(
        jnp.concatenate(
            [
                w_own,
                lax.ppermute(w_own, "c", PAIR),
                gate_pair,
                up_pair,
                lax.ppermute(gate_pair, "c", PAIR),
                lax.ppermute(up_pair, "c", PAIR),
            ],
            axis=0,
        )
    )
    d_own = down[0]
    d_own_other = lax.ppermute(d_own, "c", PAIR)
    d_later, up_pair = lax.optimization_barrier((d_own, up_pair))
    d_pair = lax.ppermute(d_later, "p", PAIR)

    ids = of_class(expert_ids.reshape(far * 4, group_rows, -1), core)
    gates = of_class(gate_weights.reshape(far * 4, group_rows, -1), core)

    def by_row(values):
        values = values.reshape(far, chips, 2, own).transpose(1, 2, 0, 3)
        return values.reshape(class_rows)

    slot_index = jnp.arange(class_slots, dtype=jnp.int32)
    hits, combine = [], []
    for expert in (plane_index * 2 + core, plane_index * 2 + 1 - core):
        slots, weights = routing(ids, gates, capacity, expert)
        hit = by_row(slots)[:, None] == slot_index[None, :]
        hits.append(hit.astype(jnp.bfloat16))
        combine.append(jnp.where(hit, by_row(weights)[:, None], 0.0).astype(jnp.bfloat16))
    combine = jnp.concatenate(combine, axis=1)

    both = lax.dot_general(
        w_all, every, (((1,), (1,)), ((), ())), preferred_element_type=jnp.float32
    )
    both = both.reshape(2, 2, 2, units, class_rows)
    hidden = (jax.nn.silu(both[:, :, 0]) * both[:, :, 1]).astype(jnp.bfloat16)
    d_pair, hidden = lax.optimization_barrier((d_pair, hidden))
    d_all = [[d_own, d_pair], [d_own_other, lax.ppermute(d_pair, "c", PAIR)]]

    outputs = []
    for e in range(2):
        picked = lax.dot_general(
            hidden[:, e].reshape(2 * units, class_rows),
            hits[e],
            (((1,), (0,)), ((), ())),
            preferred_element_type=jnp.float32,
        ).astype(jnp.bfloat16)
        picked = picked.reshape(2, units, class_slots)
        picked = jnp.where(p == 0, picked, picked[::-1]).reshape(2 * units, class_slots)
        all_hidden = lax.all_gather(picked, ("zh", "k"), axis=0, tiled=True)
        outputs.append(
            jnp.concatenate(
                [
                    lax.dot_general(
                        all_hidden, d, (((0,), (0,)), ((), ())), preferred_element_type=jnp.float32
                    ).astype(jnp.bfloat16)
                    for d in d_all[e]
                ],
                axis=1,
            )
        )
    outputs = jnp.concatenate(outputs, axis=0)

    summed = jnp.dot(combine, outputs, preferred_element_type=jnp.float32).astype(jnp.bfloat16)
    arrived = lax.all_to_all(summed, PLANE, split_axis=0, concat_axis=0, tiled=True)
    arrived = arrived.reshape(chips, 2 * far * own, arrived.shape[1]).astype(jnp.float32)
    rows = jnp.sum(arrived, axis=0).astype(jnp.bfloat16)
    features = rows.shape[1]

    rows = rows.reshape(2, far, own, features).transpose(1, 0, 2, 3)[:, None]
    here = (jnp.arange(2) == core)[None, :, None, None, None]
    send = jnp.where(here, rows, jnp.zeros((), rows.dtype)).reshape(far * 4 * own, features)
    recv = lax.all_to_all(send, ("zh", "k", "c"), split_axis=0, concat_axis=0, tiled=True)
    recv = recv.reshape(far, 2, 2, own, features)
    recv = lax.dynamic_index_in_dim(recv, k, 2, keepdims=False)
    recv = recv.reshape(far, 2, own, 2, features // 2)
    recv = jnp.where(p == 0, recv, recv[:, :, :, ::-1])
    return recv.transpose(2, 0, 1, 3, 4).reshape(own, width)


def solution(mesh):
    rows, cols = mesh.devices.shape
    side = 4
    shape = (rows // 4, 2, 2, side, cols // (2 * side), 2)
    fine = Mesh(mesh.devices.reshape(shape), LINE + PLANE + ("c",))
    row, col = LINE, PLANE + ("c",)
    in_specs = (
        P(row + col, None),
        P(col, None, row, None),
        P(col, None, row),
        P(),
        P(),
        P(),
    )
    out_specs = P(row + col, None)
    return jax.shard_map(local, mesh=fine, in_specs=in_specs, out_specs=out_specs, check_vma=False)
```

```python
import jax
import jax.numpy as jnp
from jax import lax
from jax.sharding import Mesh, PartitionSpec as P

SLOTS = 48
LINE = ("zh", "k", "p")
PLANE = ("x", "y")
PAIR = [(0, 1), (1, 0)]


def routing(expert_ids, gate_weights, capacity, expert):
    member = expert_ids == expert
    hits = jnp.sum(member.astype(jnp.int32), axis=2)
    rank = jnp.cumsum(hits, axis=1) - hits
    cap = lax.dynamic_index_in_dim(capacity, expert, 0, keepdims=False)
    weights = jnp.sum(jnp.where(member, gate_weights, 0.0), axis=2)
    offset = jnp.arange(hits.shape[0], dtype=jnp.int32)[:, None] * SLOTS
    return jnp.where((hits > 0) & (rank < cap), rank + offset, -1), weights


def local(tokens, gate_up, down, expert_ids, gate_weights, capacity):
    core = lax.axis_index("c")
    k, p = lax.axis_index("k"), lax.axis_index("p")
    plane_index = lax.axis_index(PLANE)
    chips = lax.axis_size("x") * lax.axis_size("y")
    far = lax.axis_size("zh")
    own, width = tokens.shape
    group_rows = chips * 2 * own
    class_rows = far * group_rows
    class_slots = far * SLOTS

    def of_class(values, which):
        values = values.reshape((far, 2, 2) + values.shape[1:])
        return lax.dynamic_index_in_dim(
            lax.dynamic_index_in_dim(values, p, 2, keepdims=False), which, 1, keepdims=False
        )

    units = gate_up.shape[2]
    w_own = gate_up[0].reshape(2 * units, width)
    gate_pair = lax.ppermute(w_own[:units], "p", PAIR)
    line = lax.all_gather(tokens, LINE, axis=0, tiled=False)
    mine = of_class(line, core)
    got = lax.ppermute(of_class(line, 1 - core), "c", PAIR)
    first = core == 0
    up_pair = lax.ppermute(w_own[units:], "p", PAIR)

    chip_rows = jnp.stack([jnp.where(first, mine, got), jnp.where(first, got, mine)])
    chip_rows = chip_rows.reshape(2 * far * own, width)
    every = lax.all_gather(chip_rows, PLANE, axis=0, tiled=True)

    w_all = lax.optimization_barrier(
        jnp.concatenate(
            [
                w_own,
                lax.ppermute(w_own, "c", PAIR),
                gate_pair,
                up_pair,
                lax.ppermute(gate_pair, "c", PAIR),
                lax.ppermute(up_pair, "c", PAIR),
            ],
            axis=0,
        )
    )
    d_own = down[0]
    d_own_other = lax.ppermute(d_own, "c", PAIR)
    d_later, up_pair = lax.optimization_barrier((d_own, up_pair))
    d_pair = lax.ppermute(d_later, "p", PAIR)

    ids = of_class(expert_ids.reshape(far * 4, group_rows, -1), core)
    gates = of_class(gate_weights.reshape(far * 4, group_rows, -1), core)

    def by_row(values):
        values = values.reshape(far, chips, 2, own).transpose(1, 2, 0, 3)
        return values.reshape(class_rows)

    slot_index = jnp.arange(class_slots, dtype=jnp.int32)
    hits, combine = [], []
    for expert in (plane_index * 2 + core, plane_index * 2 + 1 - core):
        slots, weights = routing(ids, gates, capacity, expert)
        hit = by_row(slots)[:, None] == slot_index[None, :]
        hits.append(hit.astype(jnp.bfloat16))
        combine.append(jnp.where(hit, by_row(weights)[:, None], 0.0).astype(jnp.bfloat16))
    combine = jnp.concatenate(combine, axis=1)

    both = lax.dot_general(
        w_all, every, (((1,), (1,)), ((), ())), preferred_element_type=jnp.float32
    )
    both = both.reshape(2, 2, 2, units, class_rows)
    hidden = (jax.nn.silu(both[:, :, 0]) * both[:, :, 1]).astype(jnp.bfloat16)
    d_pair, hidden = lax.optimization_barrier((d_pair, hidden))
    d_all = [[d_own, d_pair], [d_own_other, lax.ppermute(d_pair, "c", PAIR)]]

    outputs = []
    for e in range(2):
        picked = lax.dot_general(
            hidden[:, e].reshape(2 * units, class_rows),
            hits[e],
            (((1,), (0,)), ((), ())),
            preferred_element_type=jnp.float32,
        ).astype(jnp.bfloat16)
        picked = picked.reshape(2, units, class_slots)
        picked = jnp.where(p == 0, picked, picked[::-1]).reshape(2 * units, class_slots)
        all_hidden = lax.all_gather(picked, ("zh", "k"), axis=0, tiled=True)
        outputs.append(
            jnp.concatenate(
                [
                    lax.dot_general(
                        all_hidden, d, (((0,), (0,)), ((), ())), preferred_element_type=jnp.float32
                    ).astype(jnp.bfloat16)
                    for d in d_all[e]
                ],
                axis=1,
            )
        )
    outputs = jnp.concatenate(outputs, axis=0)

    summed = jnp.dot(combine, outputs, preferred_element_type=jnp.float32).astype(jnp.bfloat16)
    arrived = lax.all_to_all(summed, PLANE, split_axis=0, concat_axis=0, tiled=True)
    arrived = arrived.reshape(chips, 2 * far * own, arrived.shape[1]).astype(jnp.float32)
    rows = jnp.sum(arrived, axis=0).astype(jnp.bfloat16)
    features = rows.shape[1]

    rows = rows.reshape(2, far, own, features).transpose(1, 0, 2, 3)[:, None]
    here = (jnp.arange(2) == core)[None, :, None, None, None]
    send = jnp.where(here, rows, jnp.zeros((), rows.dtype)).reshape(far * 4 * own, features)
    recv = lax.all_to_all(send, ("zh", "k", "c"), split_axis=0, concat_axis=0, tiled=True)
    recv = recv.reshape(far, 2, 2, own, features)
    recv = lax.dynamic_index_in_dim(recv, k, 2, keepdims=False)
    recv = recv.reshape(far, 2, own, 2, features // 2)
    recv = jnp.where(p == 0, recv, recv[:, :, :, ::-1])
    return recv.transpose(2, 0, 1, 3, 4).reshape(own, width)


def solution(mesh):
    rows, cols = mesh.devices.shape
    side = 4
    shape = (rows // 4, 2, 2, side, cols // (2 * side), 2)
    fine = Mesh(mesh.devices.reshape(shape), LINE + PLANE + ("c",))
    row, col = LINE, PLANE + ("c",)
    in_specs = (
        P(row + col, None),
        P(col, None, row, None),
        P(col, None, row),
        P(),
        P(),
        P(),
    )
    out_specs = P(row + col, None)
    return jax.shard_map(local, mesh=fine, in_specs=in_specs, out_specs=out_specs, check_vma=False)
```

```python
import jax
import jax.numpy as jnp
from jax import lax
from jax.sharding import Mesh, PartitionSpec as P

SLOTS = 48
LINE = ("zh", "k", "p")
RING = ("zh", "k")
PLANE = ("x", "y")
PAIR = [(0, 1), (1, 0)]


def routing(expert_ids, gate_weights, capacity, expert):
    member = expert_ids == expert
    hits = jnp.sum(member.astype(jnp.int32), axis=2)
    rank = jnp.cumsum(hits, axis=1) - hits
    cap = lax.dynamic_index_in_dim(capacity, expert, 0, keepdims=False)
    weights = jnp.sum(jnp.where(member, gate_weights, 0.0), axis=2)
    offset = jnp.arange(hits.shape[0], dtype=jnp.int32)[:, None] * SLOTS
    return jnp.where((hits > 0) & (rank < cap), rank + offset, -1), weights


def local(tokens, gate_up, down, expert_ids, gate_weights, capacity):
    core = lax.axis_index("c")
    k, p = lax.axis_index("k"), lax.axis_index("p")
    plane_index = lax.axis_index(PLANE)
    chips = lax.axis_size("x") * lax.axis_size("y")
    far = lax.axis_size("zh")
    own, width = tokens.shape
    group_rows = chips * 2 * own
    class_rows = far * group_rows
    class_slots = far * SLOTS

    def of_class(values, which):
        values = values.reshape((far, 2, 2) + values.shape[1:])
        return lax.dynamic_index_in_dim(
            lax.dynamic_index_in_dim(values, p, 2, keepdims=False), which, 1, keepdims=False
        )

    units = gate_up.shape[2]
    w_own = gate_up[0].reshape(2 * units, width)
    w_pair = lax.ppermute(w_own, "p", PAIR)

    line = lax.all_gather(tokens, RING, axis=0, tiled=False).reshape(far, 2, own, width)
    mine = lax.dynamic_index_in_dim(line, core, 1, keepdims=False)
    got = lax.ppermute(lax.dynamic_index_in_dim(line, 1 - core, 1, keepdims=False), "c", PAIR)
    first = core == 0
    chip_rows = jnp.stack([jnp.where(first, mine, got), jnp.where(first, got, mine)])
    chip_rows = chip_rows.reshape(2 * far * own, width)
    every = lax.all_gather(chip_rows, PLANE, axis=0, tiled=True)

    w_other = lax.ppermute(w_own, "c", PAIR)
    w_pair_other = lax.ppermute(w_pair, "c", PAIR)
    d_own = down[0]
    d_own_other = lax.ppermute(d_own, "c", PAIR)
    d_later, w_pair = lax.optimization_barrier((d_own, w_pair))
    d_pair = lax.ppermute(d_later, "p", PAIR)

    ids = of_class(expert_ids.reshape(far * 4, group_rows, -1), core)
    gates = of_class(gate_weights.reshape(far * 4, group_rows, -1), core)

    def by_row(values):
        values = values.reshape(far, chips, 2, own).transpose(1, 2, 0, 3)
        return values.reshape(class_rows)

    slot_index = jnp.arange(class_slots, dtype=jnp.int32)
    hits, combine = [], []
    for expert in (plane_index * 2 + core, plane_index * 2 + 1 - core):
        slots, weights = routing(ids, gates, capacity, expert)
        hit = by_row(slots)[:, None] == slot_index[None, :]
        hits.append(hit.astype(jnp.bfloat16))
        combine.append(jnp.where(hit, by_row(weights)[:, None], 0.0).astype(jnp.bfloat16))
    combine = jnp.concatenate(combine, axis=1)

    def hidden_of(w):
        both = lax.dot_general(
            w, every, (((1,), (1,)), ((), ())), preferred_element_type=jnp.float32
        )
        return (jax.nn.silu(both[:units]) * both[units:]).astype(jnp.bfloat16)

    near = [hidden_of(w) for w in (w_own, w_other)]
    far_z = [hidden_of(w) for w in (w_pair, w_pair_other)]
    hidden = [jnp.concatenate([near[e], far_z[e]], axis=0) for e in range(2)]
    picked = jnp.concatenate(
        [
            jnp.dot(hidden[e], hits[e], preferred_element_type=jnp.float32).astype(jnp.bfloat16)
            for e in range(2)
        ],
        axis=1,
    )
    picked = jnp.where(p == 0, picked, jnp.roll(picked, units, axis=0))
    d_pair, picked = lax.optimization_barrier((d_pair, picked))
    d_pair_other = lax.ppermute(d_pair, "c", PAIR)

    most = 2 * units * 7 // 8
    members = far * 2
    rest = jnp.broadcast_to(picked[most:], (members, 2 * units - most, 2 * class_slots))
    rest = lax.all_to_all(rest, RING, split_axis=0, concat_axis=0, tiled=True)
    main = lax.all_gather(picked[:most], RING, axis=0, tiled=False)
    all_hidden = jnp.concatenate([main, rest], axis=1).reshape(-1, 2 * class_slots)

    outputs = []
    for e, ds in enumerate([(d_own, d_pair), (d_own_other, d_pair_other)]):
        of_expert = all_hidden[:, e * class_slots : (e + 1) * class_slots]
        outputs.append(
            jnp.concatenate(
                [
                    lax.dot_general(
                        of_expert, d, (((0,), (0,)), ((), ())), preferred_element_type=jnp.float32
                    ).astype(jnp.bfloat16)
                    for d in ds
                ],
                axis=1,
            )
        )
    outputs = jnp.concatenate(outputs, axis=0)

    summed = jnp.dot(combine, outputs, preferred_element_type=jnp.float32).astype(jnp.bfloat16)
    arrived = lax.all_to_all(summed, PLANE, split_axis=0, concat_axis=0, tiled=True)
    arrived = arrived.reshape(chips, 2 * far * own, arrived.shape[1]).astype(jnp.float32)
    rows = jnp.sum(arrived, axis=0).astype(jnp.bfloat16)
    features = rows.shape[1]

    rows = rows.reshape(2, far, own, features).transpose(1, 0, 2, 3)[:, None]
    here = (jnp.arange(2) == core)[None, :, None, None, None]
    send = jnp.where(here, rows, jnp.zeros((), rows.dtype)).reshape(far * 4 * own, features)
    recv = lax.all_to_all(send, ("zh", "k", "c"), split_axis=0, concat_axis=0, tiled=True)
    recv = recv.reshape(far, 2, 2, own, features)
    recv = lax.dynamic_index_in_dim(recv, k, 2, keepdims=False)
    recv = recv.reshape(far, 2, own, 2, features // 2)
    recv = jnp.where(p == 0, recv, recv[:, :, :, ::-1])
    return recv.transpose(2, 0, 1, 3, 4).reshape(own, width)


def solution(mesh):
    rows, cols = mesh.devices.shape
    side = 4
    shape = (rows // 4, 2, 2, side, cols // (2 * side), 2)
    fine = Mesh(mesh.devices.reshape(shape), LINE + PLANE + ("c",))
    row, col = LINE, PLANE + ("c",)
    in_specs = (
        P(row + col, None),
        P(col, None, row, None),
        P(col, None, row),
        P(),
        P(),
        P(),
    )
    out_specs = P(row + col, None)
    return jax.shard_map(local, mesh=fine, in_specs=in_specs, out_specs=out_specs, check_vma=False)
```

```python
import jax
import jax.numpy as jnp
from jax import lax
from jax.experimental import pallas as pl
from jax.experimental.pallas import tpu as pltpu
from jax.sharding import Mesh, PartitionSpec as P

SLOTS = 48
LINE = ("zh", "k", "p")
RING = ("zh", "k")
PLANE = ("x", "y")
PAIR = [(0, 1), (1, 0)]


def routing(expert_ids, gate_weights, capacity, expert):
    member = expert_ids == expert
    hits = jnp.sum(member.astype(jnp.int32), axis=2)
    rank = jnp.cumsum(hits, axis=1) - hits
    cap = lax.dynamic_index_in_dim(capacity, expert, 0, keepdims=False)
    weights = jnp.sum(jnp.where(member, gate_weights, 0.0), axis=2)
    offset = jnp.arange(hits.shape[0], dtype=jnp.int32)[:, None] * SLOTS
    return jnp.where((hits > 0) & (rank < cap), rank + offset, -1), weights


def hidden_kernel(p_ref, own_a, pair_a, own_b, pair_b, tokens, hits, out, total):
    step = pl.program_id(0)

    @pl.when(step == 0)
    def _():
        total[...] = jnp.zeros_like(total)

    w = jnp.concatenate([own_a[...], pair_a[...], own_b[...], pair_b[...]], axis=0)
    total[...] += lax.dot_general(
        w, tokens[...], (((1,), (1,)), ((), ())), preferred_element_type=jnp.float32
    )

    @pl.when(step == pl.num_programs(0) - 1)
    def _():
        rows = own_a.shape[0]
        units = rows // 2
        for z in range(2):
            hidden = []
            for expert in range(2):
                base = (2 * expert + z) * rows
                gate = total[base : base + units]
                up = total[base + units : base + rows]
                hidden.append((gate / (1.0 + jnp.exp(-gate)) * up).astype(jnp.bfloat16))
            picked = jnp.dot(
                jnp.concatenate(hidden, axis=1), hits[...], preferred_element_type=jnp.float32
            )
            place = p_ref[0] if z == 0 else 1 - p_ref[0]
            out[pl.ds(pl.multiple_of(place * units, 16), units), :] = picked.astype(jnp.bfloat16)


def slotted_hidden(p, own_a, pair_a, own_b, pair_b, tokens, hits):
    rows, width = own_a.shape
    count, slots = tokens.shape[0], hits.shape[1]
    depth = 1024 if width % 1024 == 0 else width
    weights = pl.BlockSpec((rows, depth), lambda i, p: (0, i))
    return pl.pallas_call(
        hidden_kernel,
        grid_spec=pltpu.PrefetchScalarGridSpec(
            num_scalar_prefetch=1,
            grid=(width // depth,),
            in_specs=[weights] * 4
            + [
                pl.BlockSpec((count, depth), lambda i, p: (0, i)),
                pl.BlockSpec(hits.shape, lambda i, p: (0, 0)),
            ],
            out_specs=pl.BlockSpec((rows, slots), lambda i, p: (0, 0)),
            scratch_shapes=[pltpu.VMEM((4 * rows, count), jnp.float32)],
        ),
        out_shape=jax.ShapeDtypeStruct((rows, slots), jnp.bfloat16),
        compiler_params=pltpu.CompilerParams(vmem_limit_bytes=40 * 2**20),
        cost_estimate=pl.CostEstimate(
            flops=2 * 4 * rows * width * count,
            bytes_accessed=2 * width * (4 * rows + count),
            transcendentals=2 * rows * count,
        ),
    )(p.reshape(1), own_a, pair_a, own_b, pair_b, tokens, hits)


def output_kernel(main, rest, own_a, pair_a, own_b, pair_b, combine, out):
    members = main.shape[0]
    pieces = []
    for i in range(members):
        pieces += [main[i], rest[i]]
    hidden = jnp.concatenate(pieces, axis=0)
    slots = hidden.shape[1]
    for z, (d_a, d_b) in enumerate([(own_a, own_b), (pair_a, pair_b)]):
        of_a = jnp.dot(d_a[...], hidden, preferred_element_type=jnp.float32)
        of_b = jnp.dot(d_b[...], hidden, preferred_element_type=jnp.float32)
        is_a = lax.broadcasted_iota(jnp.int32, of_a.shape, 1) < slots // 2
        outputs = jnp.where(is_a, of_a, of_b).astype(jnp.bfloat16)
        summed = lax.dot_general(
            combine[...], outputs, (((1,), (1,)), ((), ())), preferred_element_type=jnp.float32
        )
        out[:, z] = summed.astype(jnp.bfloat16).reshape(out.shape[0], out.shape[2], out.shape[3])


def token_sums(main, rest, own_a, pair_a, own_b, pair_b, combine, chips):
    features, count = own_a.shape[0], combine.shape[0]
    return pl.pallas_call(
        output_kernel,
        in_specs=[pl.BlockSpec(memory_space=pltpu.VMEM)] * 7,
        out_specs=pl.BlockSpec(memory_space=pltpu.VMEM),
        out_shape=jax.ShapeDtypeStruct((chips, 2, count // chips, features), jnp.bfloat16),
        compiler_params=pltpu.CompilerParams(vmem_limit_bytes=40 * 2**20),
        cost_estimate=pl.CostEstimate(
            flops=8 * features * own_a.shape[1] * combine.shape[1],
            bytes_accessed=8 * features * own_a.shape[1],
            transcendentals=0,
        ),
    )(main, rest, own_a, pair_a, own_b, pair_b, combine)


def local(tokens, gate_up, down, expert_ids, gate_weights, capacity):
    core = lax.axis_index("c")
    k, p = lax.axis_index("k"), lax.axis_index("p")
    plane_index = lax.axis_index(PLANE)
    chips = lax.axis_size("x") * lax.axis_size("y")
    far = lax.axis_size("zh")
    own, width = tokens.shape
    group_rows = chips * 2 * own
    class_rows = far * group_rows
    class_slots = far * SLOTS

    def of_class(values, which):
        values = values.reshape((far, 2, 2) + values.shape[1:])
        return lax.dynamic_index_in_dim(
            lax.dynamic_index_in_dim(values, p, 2, keepdims=False), which, 1, keepdims=False
        )

    units = gate_up.shape[2]
    w_own = gate_up[0].reshape(2 * units, width)
    w_pair = lax.ppermute(w_own, "p", PAIR)

    line = lax.all_gather(tokens, RING, axis=0, tiled=False).reshape(far, 2, own, width)
    mine = lax.dynamic_index_in_dim(line, core, 1, keepdims=False)
    got = lax.ppermute(lax.dynamic_index_in_dim(line, 1 - core, 1, keepdims=False), "c", PAIR)
    first = core == 0
    chip_rows = jnp.stack([jnp.where(first, mine, got), jnp.where(first, got, mine)])
    chip_rows = chip_rows.reshape(2 * far * own, width)
    every = lax.all_gather(chip_rows, PLANE, axis=0, tiled=True)

    w_other = lax.ppermute(w_own, "c", PAIR)
    d_own = down[0].T
    d_other = lax.ppermute(d_own, "c", PAIR)
    w_pair, w_other, d_other = lax.optimization_barrier((w_pair, w_other, d_other))
    d_later, w_pair = lax.optimization_barrier((d_own, w_pair))
    d_pair = lax.ppermute(d_later, "p", PAIR)
    w_pair_other = lax.ppermute(w_pair, "c", PAIR)

    ids = of_class(expert_ids.reshape(far * 4, group_rows, -1), core)
    gates = of_class(gate_weights.reshape(far * 4, group_rows, -1), core)

    def by_row(values):
        values = values.reshape(far, chips, 2, own).transpose(1, 2, 0, 3)
        return values.reshape(class_rows)

    slot_index = jnp.arange(2 * class_slots, dtype=jnp.int32)
    hits, combine = [], []
    for e, expert in enumerate((plane_index * 2 + core, plane_index * 2 + 1 - core)):
        slots, weights = routing(ids, gates, capacity, expert)
        slots = by_row(jnp.where(slots >= 0, slots + e * class_slots, -1))
        hit = slots[:, None] == slot_index[None, :]
        hits.append(hit.astype(jnp.bfloat16))
        combine.append(jnp.where(hit, by_row(weights)[:, None], 0.0))
    hits = jnp.concatenate(hits, axis=0)
    combine = (combine[0] + combine[1]).astype(jnp.bfloat16)
    hits, combine = lax.optimization_barrier((hits, combine))

    picked = slotted_hidden(p, w_own, w_pair, w_other, w_pair_other, every, hits)

    most = 2 * units * 5 // 6
    members = far * 2
    rest = jnp.broadcast_to(picked[most:], (members, 2 * units - most, 2 * class_slots))
    rest = lax.all_to_all(rest, RING, split_axis=0, concat_axis=0, tiled=True)
    main = lax.all_gather(picked[:most], RING, axis=0, tiled=False)
    d_pair, main = lax.optimization_barrier((d_pair, main))
    d_pair_other = lax.ppermute(d_pair, "c", PAIR)
    summed = token_sums(main, rest, d_own, d_pair, d_other, d_pair_other, combine, chips)

    arrived = lax.all_to_all(summed, PLANE, split_axis=0, concat_axis=0, tiled=True)
    rows = jnp.sum(arrived.astype(jnp.float32), axis=0).astype(jnp.bfloat16)
    features = rows.shape[2]

    rows = rows.reshape(2, 2, far, own, features).transpose(2, 1, 0, 3, 4)[:, None]
    here = (jnp.arange(2) == core)[None, :, None, None, None, None]
    send = jnp.where(here, rows, jnp.zeros((), rows.dtype))
    send = send.reshape(far * 4, 2 * own, features)
    recv = lax.all_to_all(send, ("zh", "k", "c"), split_axis=0, concat_axis=0, tiled=True)
    recv = recv.reshape(far, 2, 2, 2, own, features)
    recv = lax.dynamic_index_in_dim(recv, k, 2, keepdims=False)
    recv = jnp.where(p == 0, recv, recv[:, :, ::-1])
    return recv.transpose(3, 0, 1, 2, 4).reshape(own, width)


def solution(mesh):
    rows, cols = mesh.devices.shape
    side = 4
    shape = (rows // 4, 2, 2, side, cols // (2 * side), 2)
    fine = Mesh(mesh.devices.reshape(shape), LINE + PLANE + ("c",))
    row, col = LINE, PLANE + ("c",)
    in_specs = (
        P(row + col, None),
        P(col, None, row, None),
        P(col, None, row),
        P(),
        P(),
        P(),
    )
    out_specs = P(row + col, None)
    return jax.shard_map(local, mesh=fine, in_specs=in_specs, out_specs=out_specs, check_vma=False)
```

```python
import jax
import jax.numpy as jnp
from jax import lax
from jax.experimental import pallas as pl
from jax.experimental.pallas import tpu as pltpu
from jax.sharding import Mesh, PartitionSpec as P

SLOTS = 48
LINE = ("zh", "k", "p")
RING = ("zh", "k")
PLANE = ("x", "y")
PAIR = [(0, 1), (1, 0)]


def routing(expert_ids, gate_weights, capacity, expert):
    member = expert_ids == expert
    hits = jnp.sum(member.astype(jnp.int32), axis=2)
    rank = jnp.cumsum(hits, axis=1) - hits
    cap = lax.dynamic_index_in_dim(capacity, expert, 0, keepdims=False)
    weights = jnp.sum(jnp.where(member, gate_weights, 0.0), axis=2)
    offset = jnp.arange(hits.shape[0], dtype=jnp.int32)[:, None] * SLOTS
    return jnp.where((hits > 0) & (rank < cap), rank + offset, -1), weights


def hidden_kernel(p_ref, own_a, pair_a, own_b, pair_b, tokens, hits, out, total):
    step = pl.program_id(0)

    @pl.when(step == 0)
    def _():
        total[...] = jnp.zeros_like(total)

    w = jnp.concatenate([own_a[...], pair_a[...], own_b[...], pair_b[...]], axis=0)
    total[...] += lax.dot_general(
        w, tokens[...], (((1,), (1,)), ((), ())), preferred_element_type=jnp.float32
    )

    @pl.when(step == pl.num_programs(0) - 1)
    def _():
        rows = own_a.shape[0]
        units = rows // 2
        for z in range(2):
            hidden = []
            for expert in range(2):
                base = (2 * expert + z) * rows
                gate = total[base : base + units]
                up = total[base + units : base + rows]
                hidden.append((gate / (1.0 + jnp.exp(-gate)) * up).astype(jnp.bfloat16))
            picked = jnp.dot(
                jnp.concatenate(hidden, axis=1), hits[...], preferred_element_type=jnp.float32
            )
            place = p_ref[0] if z == 0 else 1 - p_ref[0]
            out[pl.ds(pl.multiple_of(place * units, 16), units), :] = picked.astype(jnp.bfloat16)


def slotted_hidden(p, own_a, pair_a, own_b, pair_b, tokens, hits):
    rows, width = own_a.shape
    count, slots = tokens.shape[0], hits.shape[1]
    depth = width // 4
    weights = pl.BlockSpec((rows, depth), lambda i, p: (0, i))
    return pl.pallas_call(
        hidden_kernel,
        grid_spec=pltpu.PrefetchScalarGridSpec(
            num_scalar_prefetch=1,
            grid=(width // depth,),
            in_specs=[weights] * 4
            + [
                pl.BlockSpec((count, depth), lambda i, p: (0, i)),
                pl.BlockSpec(hits.shape, lambda i, p: (0, 0)),
            ],
            out_specs=pl.BlockSpec((rows, slots), lambda i, p: (0, 0)),
            scratch_shapes=[pltpu.VMEM((4 * rows, count), jnp.float32)],
        ),
        out_shape=jax.ShapeDtypeStruct((rows, slots), jnp.bfloat16),
        compiler_params=pltpu.CompilerParams(vmem_limit_bytes=60 * 2**20),
        cost_estimate=pl.CostEstimate(
            flops=2 * 4 * rows * width * count,
            bytes_accessed=2 * width * (4 * rows + count),
            transcendentals=2 * rows * count,
        ),
    )(p.reshape(1), own_a, pair_a, own_b, pair_b, tokens, hits)


def output_kernel(main, rest, own_a, pair_a, own_b, pair_b, combine, out):
    members = main.shape[0]
    pieces = []
    for i in range(members):
        pieces += [main[i], rest[i]]
    hidden = jnp.concatenate(pieces, axis=0)
    slots = hidden.shape[1]
    outputs = []
    for d_a, d_b in [(own_a, own_b), (pair_a, pair_b)]:
        of_a = jnp.dot(d_a[...], hidden, preferred_element_type=jnp.float32)
        of_b = jnp.dot(d_b[...], hidden, preferred_element_type=jnp.float32)
        is_a = lax.broadcasted_iota(jnp.int32, of_a.shape, 1) < slots // 2
        outputs.append(jnp.where(is_a, of_a, of_b).astype(jnp.bfloat16))
    outputs = jnp.concatenate(outputs, axis=0)
    out[...] = lax.dot_general(
        combine[...], outputs, (((1,), (1,)), ((), ())), preferred_element_type=jnp.float32
    ).astype(jnp.bfloat16)


def token_sums(main, rest, own_a, pair_a, own_b, pair_b, combine):
    features, count = own_a.shape[0], combine.shape[0]
    return pl.pallas_call(
        output_kernel,
        in_specs=[pl.BlockSpec(memory_space=pltpu.VMEM)] * 7,
        out_specs=pl.BlockSpec(memory_space=pltpu.VMEM),
        out_shape=jax.ShapeDtypeStruct((count, 2 * features), jnp.bfloat16),
        compiler_params=pltpu.CompilerParams(vmem_limit_bytes=40 * 2**20),
        cost_estimate=pl.CostEstimate(
            flops=8 * features * own_a.shape[1] * combine.shape[1],
            bytes_accessed=8 * features * own_a.shape[1],
            transcendentals=0,
        ),
    )(main, rest, own_a, pair_a, own_b, pair_b, combine)


def local(tokens, gate_up, down, expert_ids, gate_weights, capacity):
    core = lax.axis_index("c")
    k, p = lax.axis_index("k"), lax.axis_index("p")
    plane_index = lax.axis_index(PLANE)
    chips = lax.axis_size("x") * lax.axis_size("y")
    far = lax.axis_size("zh")
    own, width = tokens.shape
    group_rows = chips * 2 * own
    class_rows = far * group_rows
    class_slots = far * SLOTS

    def of_class(values, which):
        values = values.reshape((far, 2, 2) + values.shape[1:])
        return lax.dynamic_index_in_dim(
            lax.dynamic_index_in_dim(values, p, 2, keepdims=False), which, 1, keepdims=False
        )

    units = gate_up.shape[2]
    w_own = gate_up[0].reshape(2 * units, width)
    w_pair = lax.ppermute(w_own, "p", PAIR)

    line = lax.all_gather(tokens, RING, axis=0, tiled=False).reshape(far, 2, own, width)
    mine = lax.dynamic_index_in_dim(line, core, 1, keepdims=False)
    got = lax.ppermute(lax.dynamic_index_in_dim(line, 1 - core, 1, keepdims=False), "c", PAIR)
    first = core == 0
    chip_rows = jnp.stack([jnp.where(first, mine, got), jnp.where(first, got, mine)])
    chip_rows = chip_rows.reshape(2 * far * own, width)
    every = lax.all_gather(chip_rows, PLANE, axis=0, tiled=True)

    ids = of_class(expert_ids.reshape(far * 4, group_rows, -1), core)
    gates = of_class(gate_weights.reshape(far * 4, group_rows, -1), core)

    def by_row(values):
        values = values.reshape(far, chips, 2, own).transpose(1, 2, 0, 3)
        return values.reshape(class_rows)

    slot_index = jnp.arange(2 * class_slots, dtype=jnp.int32)
    hits, combine = [], []
    for e, expert in enumerate((plane_index * 2 + core, plane_index * 2 + 1 - core)):
        slots, weights = routing(ids, gates, capacity, expert)
        slots = by_row(jnp.where(slots >= 0, slots + e * class_slots, -1))
        hit = slots[:, None] == slot_index[None, :]
        hits.append(hit.astype(jnp.bfloat16))
        combine.append(jnp.where(hit, by_row(weights)[:, None], 0.0))
    hits = jnp.concatenate(hits, axis=0)
    combine = (combine[0] + combine[1]).astype(jnp.bfloat16)

    w_other = lax.ppermute(w_own, "c", PAIR)
    d_own = down[0].T
    d_other = lax.ppermute(d_own, "c", PAIR)
    w_pair, w_other, d_other, hits, combine = lax.optimization_barrier(
        (w_pair, w_other, d_other, hits, combine)
    )
    d_later, w_pair = lax.optimization_barrier((d_own, w_pair))
    d_pair = lax.ppermute(d_later, "p", PAIR)
    w_pair_other = lax.ppermute(w_pair, "c", PAIR)

    picked = slotted_hidden(p, w_own, w_pair, w_other, w_pair_other, every, hits)

    most = 2 * units * 5 // 6
    members = far * 2
    rest = jnp.broadcast_to(picked[most:], (members, 2 * units - most, 2 * class_slots))
    rest = lax.all_to_all(rest, RING, split_axis=0, concat_axis=0, tiled=True)
    main = lax.all_gather(picked[:most], RING, axis=0, tiled=False)
    d_pair, main, rest = lax.optimization_barrier((d_pair, main, rest))
    d_pair_other = lax.ppermute(d_pair, "c", PAIR)
    summed = token_sums(main, rest, d_own, d_pair, d_other, d_pair_other, combine)

    arrived = lax.all_to_all(summed, PLANE, split_axis=0, concat_axis=0, tiled=True)
    arrived = arrived.reshape(chips, 2 * far * own, arrived.shape[1]).astype(jnp.float32)
    rows = jnp.sum(arrived, axis=0).astype(jnp.bfloat16)
    features = rows.shape[1]

    rows = rows.reshape(2, far, own, features).transpose(1, 0, 2, 3)[:, None]
    here = (jnp.arange(2) == core)[None, :, None, None, None]
    send = jnp.where(here, rows, jnp.zeros((), rows.dtype)).reshape(far * 4 * own, features)
    recv = lax.all_to_all(send, ("zh", "k", "c"), split_axis=0, concat_axis=0, tiled=True)
    recv = recv.reshape(far, 2, 2, own, features)
    recv = lax.dynamic_index_in_dim(recv, k, 2, keepdims=False)
    recv = recv.reshape(far, 2, own, 2, features // 2)
    recv = jnp.where(p == 0, recv, recv[:, :, :, ::-1])
    return recv.transpose(2, 0, 1, 3, 4).reshape(own, width)


def solution(mesh):
    rows, cols = mesh.devices.shape
    side = 4
    shape = (rows // 4, 2, 2, side, cols // (2 * side), 2)
    fine = Mesh(mesh.devices.reshape(shape), LINE + PLANE + ("c",))
    row, col = LINE, PLANE + ("c",)
    in_specs = (
        P(row + col, None),
        P(col, None, row, None),
        P(col, None, row),
        P(),
        P(),
        P(),
    )
    out_specs = P(row + col, None)
    return jax.shard_map(local, mesh=fine, in_specs=in_specs, out_specs=out_specs, check_vma=False)
```

```python
import jax
import jax.numpy as jnp
from jax import lax
from jax.experimental import pallas as pl
from jax.experimental.pallas import tpu as pltpu
from jax.sharding import Mesh, PartitionSpec as P

SLOTS = 48
LINE = ("zh", "k", "p")
RING = ("zh", "k")
PLANE = ("x", "y")
PAIR = [(0, 1), (1, 0)]


def routing(expert_ids, gate_weights, capacity, expert):
    member = expert_ids == expert
    hits = jnp.sum(member.astype(jnp.int32), axis=2)
    rank = jnp.cumsum(hits, axis=1) - hits
    cap = lax.dynamic_index_in_dim(capacity, expert, 0, keepdims=False)
    weights = jnp.sum(jnp.where(member, gate_weights, 0.0), axis=2)
    offset = jnp.arange(hits.shape[0], dtype=jnp.int32)[:, None] * SLOTS
    return jnp.where((hits > 0) & (rank < cap), rank + offset, -1), weights


def hidden_kernel(p_ref, own_a, pair_a, own_b, pair_b, tokens, hits, out, total):
    step = pl.program_id(0)

    @pl.when(step == 0)
    def _():
        total[...] = jnp.zeros_like(total)

    w = jnp.concatenate([own_a[...], pair_a[...], own_b[...], pair_b[...]], axis=0)
    total[...] += lax.dot_general(
        w, tokens[...], (((1,), (1,)), ((), ())), preferred_element_type=jnp.float32
    )

    @pl.when(step == pl.num_programs(0) - 1)
    def _():
        rows = own_a.shape[0]
        units = rows // 2
        for z in range(2):
            hidden = []
            for expert in range(2):
                base = (2 * expert + z) * rows
                gate = total[base : base + units]
                up = total[base + units : base + rows]
                hidden.append((gate / (1.0 + jnp.exp(-gate)) * up).astype(jnp.bfloat16))
            picked = jnp.dot(
                jnp.concatenate(hidden, axis=1), hits[...], preferred_element_type=jnp.float32
            )
            place = p_ref[0] if z == 0 else 1 - p_ref[0]
            out[pl.ds(pl.multiple_of(place * units, 16), units), :] = picked.astype(jnp.bfloat16)


def slotted_hidden(p, own_a, pair_a, own_b, pair_b, tokens, hits):
    rows, width = own_a.shape
    count, slots = tokens.shape[0], hits.shape[1]
    depth = width // 4
    weights = pl.BlockSpec((rows, depth), lambda i, p: (0, i))
    return pl.pallas_call(
        hidden_kernel,
        grid_spec=pltpu.PrefetchScalarGridSpec(
            num_scalar_prefetch=1,
            grid=(width // depth,),
            in_specs=[weights] * 4
            + [
                pl.BlockSpec((count, depth), lambda i, p: (0, i)),
                pl.BlockSpec(hits.shape, lambda i, p: (0, 0)),
            ],
            out_specs=pl.BlockSpec((rows, slots), lambda i, p: (0, 0)),
            scratch_shapes=[pltpu.VMEM((4 * rows, count), jnp.float32)],
        ),
        out_shape=jax.ShapeDtypeStruct((rows, slots), jnp.bfloat16),
        compiler_params=pltpu.CompilerParams(vmem_limit_bytes=60 * 2**20),
        cost_estimate=pl.CostEstimate(
            flops=2 * 4 * rows * width * count,
            bytes_accessed=2 * width * (4 * rows + count),
            transcendentals=2 * rows * count,
        ),
    )(p.reshape(1), own_a, pair_a, own_b, pair_b, tokens, hits)


def output_kernel(main, rest, own_a, pair_a, own_b, pair_b, combine, out):
    members = main.shape[0]
    pieces = []
    for i in range(members):
        pieces += [main[i], rest[i]]
    hidden = jnp.concatenate(pieces, axis=0)
    slots = hidden.shape[1]
    outputs = []
    for d_a, d_b in [(own_a, own_b), (pair_a, pair_b)]:
        of_a = jnp.dot(d_a[...], hidden, preferred_element_type=jnp.float32)
        of_b = jnp.dot(d_b[...], hidden, preferred_element_type=jnp.float32)
        is_a = lax.broadcasted_iota(jnp.int32, of_a.shape, 1) < slots // 2
        outputs.append(jnp.where(is_a, of_a, of_b).astype(jnp.bfloat16))
    outputs = jnp.concatenate(outputs, axis=0)
    out[...] = lax.dot_general(
        combine[...], outputs, (((1,), (1,)), ((), ())), preferred_element_type=jnp.float32
    ).astype(jnp.bfloat16)


def token_sums(main, rest, own_a, pair_a, own_b, pair_b, combine):
    features, count = own_a.shape[0], combine.shape[0]
    return pl.pallas_call(
        output_kernel,
        in_specs=[pl.BlockSpec(memory_space=pltpu.VMEM)] * 7,
        out_specs=pl.BlockSpec(memory_space=pltpu.VMEM),
        out_shape=jax.ShapeDtypeStruct((count, 2 * features), jnp.bfloat16),
        compiler_params=pltpu.CompilerParams(vmem_limit_bytes=40 * 2**20),
        cost_estimate=pl.CostEstimate(
            flops=8 * features * own_a.shape[1] * combine.shape[1],
            bytes_accessed=8 * features * own_a.shape[1],
            transcendentals=0,
        ),
    )(main, rest, own_a, pair_a, own_b, pair_b, combine)


def local(tokens, gate_up, down, expert_ids, gate_weights, capacity):
    core = lax.axis_index("c")
    k, p = lax.axis_index("k"), lax.axis_index("p")
    plane_index = lax.axis_index(PLANE)
    chips = lax.axis_size("x") * lax.axis_size("y")
    far = lax.axis_size("zh")
    own, width = tokens.shape
    group_rows = chips * 2 * own
    class_rows = far * group_rows
    class_slots = far * SLOTS

    def of_class(values, which):
        values = values.reshape((far, 2, 2) + values.shape[1:])
        return lax.dynamic_index_in_dim(
            lax.dynamic_index_in_dim(values, p, 2, keepdims=False), which, 1, keepdims=False
        )

    units = gate_up.shape[2]
    w_own = gate_up[0].reshape(2 * units, width)
    w_pair = lax.ppermute(w_own, "p", PAIR)

    line = lax.all_gather(tokens, RING, axis=0, tiled=False).reshape(far, 2, own, width)
    mine = lax.dynamic_index_in_dim(line, core, 1, keepdims=False)
    got = lax.ppermute(lax.dynamic_index_in_dim(line, 1 - core, 1, keepdims=False), "c", PAIR)
    first = core == 0
    chip_rows = jnp.stack([jnp.where(first, mine, got), jnp.where(first, got, mine)])
    chip_rows = chip_rows.reshape(2 * far * own, width)
    every = lax.all_gather(chip_rows, PLANE, axis=0, tiled=True)

    ids = of_class(expert_ids.reshape(far * 4, group_rows, -1), core)
    gates = of_class(gate_weights.reshape(far * 4, group_rows, -1), core)

    def by_row(values):
        values = values.reshape(far, chips, 2, own).transpose(1, 2, 0, 3)
        return values.reshape(class_rows)

    slot_index = jnp.arange(2 * class_slots, dtype=jnp.int32)
    hits, combine = [], []
    for e, expert in enumerate((plane_index * 2 + core, plane_index * 2 + 1 - core)):
        slots, weights = routing(ids, gates, capacity, expert)
        slots = by_row(jnp.where(slots >= 0, slots + e * class_slots, -1))
        hit = slots[:, None] == slot_index[None, :]
        hits.append(hit.astype(jnp.bfloat16))
        combine.append(jnp.where(hit, by_row(weights)[:, None], 0.0))
    hits = jnp.concatenate(hits, axis=0)
    combine = (combine[0] + combine[1]).astype(jnp.bfloat16)

    w_other = lax.ppermute(w_own, "c", PAIR)
    d_own = down[0].T
    d_other = lax.ppermute(d_own, "c", PAIR)
    line = far * 4
    swap = [(z, (z + 1) % line if z % 2 else (z - 1) % line) for z in range(line)]
    d_pair = lax.ppermute(d_own, LINE, swap)
    d_pair_other = lax.ppermute(d_pair, "c", PAIR)
    w_pair, w_other, d_other, d_pair_other, hits, combine = lax.optimization_barrier(
        (w_pair, w_other, d_other, d_pair_other, hits, combine)
    )
    w_pair_other = lax.ppermute(w_pair, "c", PAIR)

    picked = slotted_hidden(p, w_own, w_pair, w_other, w_pair_other, every, hits)

    most = 2 * units * 5 // 6
    members = far * 2
    rest = jnp.broadcast_to(picked[most:], (members, 2 * units - most, 2 * class_slots))
    rest = lax.all_to_all(rest, RING, split_axis=0, concat_axis=0, tiled=True)
    main = lax.all_gather(picked[:most], RING, axis=0, tiled=False)
    summed = token_sums(main, rest, d_own, d_pair, d_other, d_pair_other, combine)

    arrived = lax.all_to_all(summed, PLANE, split_axis=0, concat_axis=0, tiled=True)
    arrived = arrived.reshape(chips, 2 * far * own, arrived.shape[1]).astype(jnp.float32)
    rows = jnp.sum(arrived, axis=0).astype(jnp.bfloat16)
    features = rows.shape[1]

    rows = rows.reshape(2, far, own, features).transpose(1, 0, 2, 3)[:, None]
    here = (jnp.arange(2) == core)[None, :, None, None, None]
    send = jnp.where(here, rows, jnp.zeros((), rows.dtype)).reshape(far * 4 * own, features)
    recv = lax.all_to_all(send, ("zh", "k", "c"), split_axis=0, concat_axis=0, tiled=True)
    recv = recv.reshape(far, 2, 2, own, features)
    recv = lax.dynamic_index_in_dim(recv, k, 2, keepdims=False)
    recv = recv.reshape(far * 2, own, 2, features // 2)
    own_z, pair_z = recv[:, :, 0], recv[:, :, 1]
    even = jnp.where(p == 0, own_z, jnp.roll(pair_z, 1, axis=0))
    odd = jnp.where(p == 0, jnp.roll(pair_z, -1, axis=0), own_z)
    return jnp.stack([even, odd], axis=1).transpose(2, 0, 1, 3).reshape(own, width)


def solution(mesh):
    rows, cols = mesh.devices.shape
    side = 4
    shape = (rows // 4, 2, 2, side, cols // (2 * side), 2)
    fine = Mesh(mesh.devices.reshape(shape), LINE + PLANE + ("c",))
    row, col = LINE, PLANE + ("c",)
    in_specs = (
        P(row + col, None),
        P(col, None, row, None),
        P(col, None, row),
        P(),
        P(),
        P(),
    )
    out_specs = P(row + col, None)
    return jax.shard_map(local, mesh=fine, in_specs=in_specs, out_specs=out_specs, check_vma=False)
```

```python
import jax
import jax.numpy as jnp
from jax import lax
from jax.experimental import pallas as pl
from jax.experimental.pallas import tpu as pltpu
from jax.sharding import Mesh, PartitionSpec as P

SLOTS = 48
LINE = ("zh", "k", "p")
RING = ("zh", "k")
PLANE = ("x", "y")
PAIR = [(0, 1), (1, 0)]


def routing(expert_ids, gate_weights, capacity, expert):
    member = expert_ids == expert
    hits = jnp.sum(member.astype(jnp.int32), axis=2)
    rank = jnp.cumsum(hits, axis=1) - hits
    cap = lax.dynamic_index_in_dim(capacity, expert, 0, keepdims=False)
    weights = jnp.sum(jnp.where(member, gate_weights, 0.0), axis=2)
    offset = jnp.arange(hits.shape[0], dtype=jnp.int32)[:, None] * SLOTS
    return jnp.where((hits > 0) & (rank < cap), rank + offset, -1), weights


def hidden_kernel(p_ref, own_a, pair_a, own_b, pair_b, tokens, hits, out, total):
    step = pl.program_id(0)

    @pl.when(step == 0)
    def _():
        total[...] = jnp.zeros_like(total)

    w = jnp.concatenate([own_a[...], pair_a[...], own_b[...], pair_b[...]], axis=0)
    total[...] += lax.dot_general(
        w, tokens[...], (((1,), (1,)), ((), ())), preferred_element_type=jnp.float32
    )

    @pl.when(step == pl.num_programs(0) - 1)
    def _():
        rows = own_a.shape[0]
        units = rows // 2
        for z in range(2):
            hidden = []
            for expert in range(2):
                base = (2 * expert + z) * rows
                gate = total[base : base + units]
                up = total[base + units : base + rows]
                hidden.append((gate / (1.0 + jnp.exp(-gate)) * up).astype(jnp.bfloat16))
            picked = jnp.dot(
                jnp.concatenate(hidden, axis=1), hits[...], preferred_element_type=jnp.float32
            )
            place = p_ref[0] if z == 0 else 1 - p_ref[0]
            out[pl.ds(pl.multiple_of(place * units, 16), units), :] = picked.astype(jnp.bfloat16)


def slotted_hidden(p, own_a, pair_a, own_b, pair_b, tokens, hits):
    rows, width = own_a.shape
    count, slots = tokens.shape[0], hits.shape[1]
    depth = width // 4
    weights = pl.BlockSpec((rows, depth), lambda i, p: (0, i))
    return pl.pallas_call(
        hidden_kernel,
        grid_spec=pltpu.PrefetchScalarGridSpec(
            num_scalar_prefetch=1,
            grid=(width // depth,),
            in_specs=[weights] * 4
            + [
                pl.BlockSpec((count, depth), lambda i, p: (0, i)),
                pl.BlockSpec(hits.shape, lambda i, p: (0, 0)),
            ],
            out_specs=pl.BlockSpec((rows, slots), lambda i, p: (0, 0)),
            scratch_shapes=[pltpu.VMEM((4 * rows, count), jnp.float32)],
        ),
        out_shape=jax.ShapeDtypeStruct((rows, slots), jnp.bfloat16),
        compiler_params=pltpu.CompilerParams(vmem_limit_bytes=60 * 2**20),
        cost_estimate=pl.CostEstimate(
            flops=2 * 4 * rows * width * count,
            bytes_accessed=2 * width * (4 * rows + count),
            transcendentals=2 * rows * count,
        ),
    )(p.reshape(1), own_a, pair_a, own_b, pair_b, tokens, hits)


def output_kernel(hidden, own_a, pair_a, own_b, pair_b, combine, out):
    cut = hidden.shape[1] // 2
    low, high = cut // 128 * 128, -(-cut // 128) * 128
    outputs = []
    for d_a, d_b in [(own_a, own_b), (pair_a, pair_b)]:
        of_a = jnp.dot(d_a[...], hidden[:, :high], preferred_element_type=jnp.float32)
        of_b = jnp.dot(d_b[...], hidden[:, low:], preferred_element_type=jnp.float32)
        pieces = [of_a[:, :low]]
        if high > low:
            middle = of_a[:, low:]
            is_a = lax.broadcasted_iota(jnp.int32, middle.shape, 1) < cut - low
            pieces.append(jnp.where(is_a, middle, of_b[:, : high - low]))
        pieces.append(of_b[:, high - low :])
        outputs.append(jnp.concatenate(pieces, axis=1).astype(jnp.bfloat16))
    outputs = jnp.concatenate(outputs, axis=0)
    out[...] = lax.dot_general(
        combine[...], outputs, (((1,), (1,)), ((), ())), preferred_element_type=jnp.float32
    ).astype(jnp.bfloat16)


def token_sums(hidden, own_a, pair_a, own_b, pair_b, combine):
    features, count = own_a.shape[0], combine.shape[0]
    return pl.pallas_call(
        output_kernel,
        in_specs=[pl.BlockSpec(memory_space=pltpu.VMEM)] * 6,
        out_specs=pl.BlockSpec(memory_space=pltpu.VMEM),
        out_shape=jax.ShapeDtypeStruct((count, 2 * features), jnp.bfloat16),
        compiler_params=pltpu.CompilerParams(vmem_limit_bytes=40 * 2**20),
        cost_estimate=pl.CostEstimate(
            flops=8 * features * own_a.shape[1] * combine.shape[1],
            bytes_accessed=8 * features * own_a.shape[1],
            transcendentals=0,
        ),
    )(hidden, own_a, pair_a, own_b, pair_b, combine)


def local(tokens, gate_up, down, expert_ids, gate_weights, capacity):
    core = lax.axis_index("c")
    k, p = lax.axis_index("k"), lax.axis_index("p")
    plane_index = lax.axis_index(PLANE)
    chips = lax.axis_size("x") * lax.axis_size("y")
    far = lax.axis_size("zh")
    own, width = tokens.shape
    group_rows = chips * 2 * own
    class_rows = far * group_rows
    class_slots = far * SLOTS

    def of_class(values, which):
        values = values.reshape((far, 2, 2) + values.shape[1:])
        return lax.dynamic_index_in_dim(
            lax.dynamic_index_in_dim(values, p, 2, keepdims=False), which, 1, keepdims=False
        )

    units = gate_up.shape[2]
    w_own = gate_up[0].reshape(2 * units, width)
    w_pair = lax.ppermute(w_own, "p", PAIR)

    chip_rows = lax.all_gather(tokens, RING + ("c",), axis=0, tiled=False)
    chip_rows = chip_rows.reshape(far, 2, 2, own, width)
    chip_rows = lax.dynamic_index_in_dim(chip_rows, core, 1, keepdims=False)
    chip_rows = chip_rows.reshape(2 * far * own, width)
    every = lax.all_gather(chip_rows, PLANE, axis=0, tiled=True)

    ids = of_class(expert_ids.reshape(far * 4, group_rows, -1), core)
    gates = of_class(gate_weights.reshape(far * 4, group_rows, -1), core)

    def by_row(values):
        values = values.reshape(far, chips, 2, own).transpose(1, 0, 2, 3)
        return values.reshape(class_rows)

    slot_index = jnp.arange(2 * class_slots, dtype=jnp.int32)
    hits, combine = [], []
    for e, expert in enumerate((plane_index * 2 + core, plane_index * 2 + 1 - core)):
        slots, weights = routing(ids, gates, capacity, expert)
        slots = by_row(jnp.where(slots >= 0, slots + e * class_slots, -1))
        hit = slots[:, None] == slot_index[None, :]
        hits.append(hit.astype(jnp.bfloat16))
        combine.append(jnp.where(hit, by_row(weights)[:, None], 0.0))
    hits = jnp.concatenate(hits, axis=0)
    combine = (combine[0] + combine[1]).astype(jnp.bfloat16)

    w_other = lax.ppermute(w_own, "c", PAIR)
    d_own = down[0].T
    d_other = lax.ppermute(d_own, "c", PAIR)
    line = far * 4
    swap = [(z, (z + 1) % line if z % 2 else (z - 1) % line) for z in range(line)]
    d_pair = lax.ppermute(d_own, LINE, swap)
    d_pair_other = lax.ppermute(d_pair, "c", PAIR)
    w_pair, w_other, d_other, d_pair_other, hits, combine = lax.optimization_barrier(
        (w_pair, w_other, d_other, d_pair_other, hits, combine)
    )
    w_pair_other = lax.ppermute(w_pair, "c", PAIR)

    picked = slotted_hidden(p, w_own, w_pair, w_other, w_pair_other, every, hits)

    all_hidden = lax.all_gather(picked, RING, axis=0, tiled=True)
    summed = token_sums(all_hidden, d_own, d_pair, d_other, d_pair_other, combine)

    arrived = lax.all_to_all(summed, PLANE, split_axis=0, concat_axis=0, tiled=True)
    arrived = arrived.reshape(chips, 2 * far * own, arrived.shape[1]).astype(jnp.float32)
    rows = jnp.sum(arrived, axis=0).astype(jnp.bfloat16)
    features = rows.shape[1]

    rows = rows.reshape(far, 2, own, features)[:, None]
    here = (jnp.arange(2) == core)[None, :, None, None, None]
    send = jnp.where(here, rows, jnp.zeros((), rows.dtype)).reshape(far * 4 * own, features)
    recv = lax.all_to_all(send, ("zh", "k", "c"), split_axis=0, concat_axis=0, tiled=True)
    recv = recv.reshape(far, 2, 2, own, features)
    recv = lax.dynamic_index_in_dim(recv, k, 2, keepdims=False)
    recv = recv.reshape(far * 2, own, 2, features // 2)
    own_z, pair_z = recv[:, :, 0], recv[:, :, 1]
    even = jnp.where(p == 0, own_z, jnp.roll(pair_z, 1, axis=0))
    odd = jnp.where(p == 0, jnp.roll(pair_z, -1, axis=0), own_z)
    return jnp.stack([even, odd], axis=1).transpose(2, 0, 1, 3).reshape(own, width)


def solution(mesh):
    rows, cols = mesh.devices.shape
    side = 4
    shape = (rows // 4, 2, 2, side, cols // (2 * side), 2)
    fine = Mesh(mesh.devices.reshape(shape), LINE + PLANE + ("c",))
    row, col = LINE, PLANE + ("c",)
    in_specs = (
        P(row + col, None),
        P(col, None, row, None),
        P(col, None, row),
        P(),
        P(),
        P(),
    )
    out_specs = P(row + col, None)
    return jax.shard_map(local, mesh=fine, in_specs=in_specs, out_specs=out_specs, check_vma=False)
```

```python
import jax
import jax.numpy as jnp
from jax import lax
from jax.experimental import pallas as pl
from jax.experimental.pallas import tpu as pltpu
from jax.sharding import Mesh, PartitionSpec as P

SLOTS = 48
LINE = ("zh", "k", "p")
RING = ("zh", "k")
PLANE = ("x", "y")
PAIR = [(0, 1), (1, 0)]


def routing(expert_ids, gate_weights, capacity, expert):
    member = expert_ids == expert
    hits = jnp.sum(member.astype(jnp.int32), axis=2)
    rank = jnp.cumsum(hits, axis=1) - hits
    cap = lax.dynamic_index_in_dim(capacity, expert, 0, keepdims=False)
    weights = jnp.sum(jnp.where(member, gate_weights, 0.0), axis=2)
    offset = jnp.arange(hits.shape[0], dtype=jnp.int32)[:, None] * SLOTS
    return jnp.where((hits > 0) & (rank < cap), rank + offset, -1), weights


def start_total(total):
    @pl.when(pl.program_id(0) == 0)
    def _():
        total[...] = jnp.zeros_like(total)


def add_product(total, rows, tokens):
    total[...] += lax.dot_general(
        jnp.concatenate(rows, axis=0),
        tokens[...],
        (((1,), (1,)), ((), ())),
        preferred_element_type=jnp.float32,
    )


def unit_values(gate, up):
    return (gate / (1.0 + jnp.exp(-gate)) * up).astype(jnp.bfloat16)


def pick(hidden, hits):
    return jnp.dot(
        jnp.concatenate(hidden, axis=1), hits[...], preferred_element_type=jnp.float32
    ).astype(jnp.bfloat16)


def rest_kernel(gate_a, up_a, gate_b, up_b, tokens, hits, out, total):
    start_total(total)
    add_product(total, [gate_a[...], up_a[...], gate_b[...], up_b[...]], tokens)

    @pl.when(pl.program_id(0) == pl.num_programs(0) - 1)
    def _():
        n = gate_a.shape[0]
        hidden = [unit_values(total[i * n : (i + 1) * n], total[(i + 1) * n : (i + 2) * n]) for i in (0, 2)]
        picked = pick(hidden, hits)
        for i in range(out.shape[0]):
            out[i] = picked


def main_kernel(own_a, pair_a, own_b, pair_b, tokens, hits, out, total):
    start_total(total)
    units = pair_a.shape[0] // 2
    kept = out.shape[0] - units
    rows = []
    for own, pair in ((own_a, pair_a), (own_b, pair_b)):
        rows += [own[:kept], own[units : units + kept], pair[...]]
    add_product(total, rows, tokens)

    @pl.when(pl.program_id(0) == pl.num_programs(0) - 1)
    def _():
        hidden = []
        for expert in range(2):
            base = expert * 2 * (kept + units)
            middle = base + 2 * kept
            near = unit_values(total[base : base + kept], total[base + kept : middle])
            far = unit_values(total[middle : middle + units], total[middle + units : middle + 2 * units])
            hidden.append(jnp.concatenate([near, far], axis=0))
        out[...] = pick(hidden, hits)


def slotted_hidden(kernel, weights, tokens, hits, total_rows, out_shape):
    count, width = tokens.shape
    depth = width // 4
    whole = lambda shape: pl.BlockSpec(shape, lambda i: (0,) * len(shape))
    return pl.pallas_call(
        kernel,
        grid=(width // depth,),
        in_specs=[pl.BlockSpec((size, depth), lambda i, at=at: (at, i)) for _, size, at in weights]
        + [pl.BlockSpec((count, depth), lambda i: (0, i)), whole(hits.shape)],
        out_specs=whole(out_shape),
        scratch_shapes=[pltpu.VMEM((total_rows, count), jnp.float32)],
        out_shape=jax.ShapeDtypeStruct(out_shape, jnp.bfloat16),
        compiler_params=pltpu.CompilerParams(vmem_limit_bytes=60 * 2**20),
        cost_estimate=pl.CostEstimate(
            flops=2 * total_rows * width * count,
            bytes_accessed=2 * width * (total_rows + count),
            transcendentals=total_rows * count // 2,
        ),
    )(*[w for w, _, _ in weights], tokens, hits)


def output_kernel(p_ref, main, rest, own_a, pair_a, own_b, pair_b, combine, out, hidden):
    members, ends = rest.shape[0], rest.shape[1]
    both = main.shape[1] + ends
    units = both // 2
    kept = units - ends
    for i in range(members):
        own = pl.multiple_of(i * both + p_ref[0] * units, ends)
        other = pl.multiple_of(i * both + (1 - p_ref[0]) * units, ends)
        hidden[pl.ds(own, kept), :] = main[i, :kept]
        hidden[pl.ds(own + kept, ends), :] = rest[i]
        hidden[pl.ds(other, units), :] = main[i, kept:]
    cut = hidden.shape[1] // 2
    low, high = cut // 128 * 128, -(-cut // 128) * 128
    outputs = []
    for d_a, d_b in [(own_a, own_b), (pair_a, pair_b)]:
        of_a = jnp.dot(d_a[...], hidden[:, :high], preferred_element_type=jnp.float32)
        of_b = jnp.dot(d_b[...], hidden[:, low:], preferred_element_type=jnp.float32)
        pieces = [of_a[:, :low]]
        if high > low:
            middle = of_a[:, low:]
            is_a = lax.broadcasted_iota(jnp.int32, middle.shape, 1) < cut - low
            pieces.append(jnp.where(is_a, middle, of_b[:, : high - low]))
        pieces.append(of_b[:, high - low :])
        outputs.append(jnp.concatenate(pieces, axis=1).astype(jnp.bfloat16))
    outputs = jnp.concatenate(outputs, axis=0)
    out[...] = lax.dot_general(
        combine[...], outputs, (((1,), (1,)), ((), ())), preferred_element_type=jnp.float32
    ).astype(jnp.bfloat16)


def token_sums(p, main, rest, own_a, pair_a, own_b, pair_b, combine):
    features, units = own_a.shape
    count, slots = combine.shape
    return pl.pallas_call(
        output_kernel,
        in_specs=[pl.BlockSpec(memory_space=pltpu.SMEM)]
        + [pl.BlockSpec(memory_space=pltpu.VMEM)] * 7,
        out_specs=pl.BlockSpec(memory_space=pltpu.VMEM),
        scratch_shapes=[pltpu.VMEM((units, slots), jnp.bfloat16)],
        out_shape=jax.ShapeDtypeStruct((count, 2 * features), jnp.bfloat16),
        compiler_params=pltpu.CompilerParams(vmem_limit_bytes=40 * 2**20),
        cost_estimate=pl.CostEstimate(
            flops=8 * features * units * slots,
            bytes_accessed=8 * features * units,
            transcendentals=0,
        ),
    )(p.reshape(1), main, rest, own_a, pair_a, own_b, pair_b, combine)


def local(tokens, gate_up, down, expert_ids, gate_weights, capacity):
    core = lax.axis_index("c")
    k, p = lax.axis_index("k"), lax.axis_index("p")
    plane_index = lax.axis_index(PLANE)
    chips = lax.axis_size("x") * lax.axis_size("y")
    far = lax.axis_size("zh")
    own, width = tokens.shape
    group_rows = chips * 2 * own
    class_rows = far * group_rows
    class_slots = far * SLOTS

    def of_class(values, which):
        values = values.reshape((far, 2, 2) + values.shape[1:])
        return lax.dynamic_index_in_dim(
            lax.dynamic_index_in_dim(values, p, 2, keepdims=False), which, 1, keepdims=False
        )

    units = gate_up.shape[2]
    w_own = gate_up[0].reshape(2 * units, width)
    w_pair = lax.ppermute(w_own, "p", PAIR)

    chip_rows = lax.all_gather(tokens, RING + ("c",), axis=0, tiled=False)
    chip_rows = chip_rows.reshape(far, 2, 2, own, width)
    chip_rows = lax.dynamic_index_in_dim(chip_rows, core, 1, keepdims=False)
    chip_rows = chip_rows.reshape(2 * far * own, width)
    every = lax.all_gather(chip_rows, PLANE, axis=0, tiled=True)

    ids = of_class(expert_ids.reshape(far * 4, group_rows, -1), core)
    gates = of_class(gate_weights.reshape(far * 4, group_rows, -1), core)

    def by_row(values):
        values = values.reshape(far, chips, 2, own).transpose(1, 0, 2, 3)
        return values.reshape(class_rows)

    slot_index = jnp.arange(2 * class_slots, dtype=jnp.int32)
    hits, combine = [], []
    for e, expert in enumerate((plane_index * 2 + core, plane_index * 2 + 1 - core)):
        slots, weights = routing(ids, gates, capacity, expert)
        slots = by_row(jnp.where(slots >= 0, slots + e * class_slots, -1))
        hit = slots[:, None] == slot_index[None, :]
        hits.append(hit.astype(jnp.bfloat16))
        combine.append(jnp.where(hit, by_row(weights)[:, None], 0.0))
    hits = jnp.concatenate(hits, axis=0)
    combine = (combine[0] + combine[1]).astype(jnp.bfloat16)

    w_other = lax.ppermute(w_own, "c", PAIR)
    d_own = down[0].T
    d_other = lax.ppermute(d_own, "c", PAIR)
    line = far * 4
    swap = [(z, (z + 1) % line if z % 2 else (z - 1) % line) for z in range(line)]
    d_pair = lax.ppermute(d_own, LINE, swap)
    d_pair_other = lax.ppermute(d_pair, "c", PAIR)
    w_pair, w_other, d_other, d_pair_other, hits, combine = lax.optimization_barrier(
        (w_pair, w_other, d_other, d_pair_other, hits, combine)
    )
    w_pair_other = lax.ppermute(w_pair, "c", PAIR)

    ends = units // 3
    kept = units - ends
    members = far * 2
    places = (kept // ends, (units + kept) // ends)
    rest = slotted_hidden(
        rest_kernel,
        [(w, ends, at) for w in (w_own, w_other) for at in places],
        every,
        hits,
        4 * ends,
        (members, ends, 2 * class_slots),
    )
    every, rest = lax.optimization_barrier((every, rest))
    rest = lax.all_to_all(rest, RING, split_axis=0, concat_axis=0, tiled=True)
    main = slotted_hidden(
        main_kernel,
        [(w, 2 * units, 0) for w in (w_own, w_pair, w_other, w_pair_other)],
        every,
        hits,
        4 * (units + kept),
        (units + kept, 2 * class_slots),
    )
    main = lax.all_gather(main, RING, axis=0, tiled=False)
    summed = token_sums(p, main, rest, d_own, d_pair, d_other, d_pair_other, combine)

    arrived = lax.all_to_all(summed, PLANE, split_axis=0, concat_axis=0, tiled=True)
    arrived = arrived.reshape(chips, 2 * far * own, arrived.shape[1]).astype(jnp.float32)
    rows = jnp.sum(arrived, axis=0).astype(jnp.bfloat16)
    features = rows.shape[1]

    rows = rows.reshape(far, 2, own, features)[:, None]
    here = (jnp.arange(2) == core)[None, :, None, None, None]
    send = jnp.where(here, rows, jnp.zeros((), rows.dtype)).reshape(far * 4 * own, features)
    recv = lax.all_to_all(send, ("zh", "k", "c"), split_axis=0, concat_axis=0, tiled=True)
    recv = recv.reshape(far, 2, 2, own, features)
    recv = lax.dynamic_index_in_dim(recv, k, 2, keepdims=False)
    recv = recv.reshape(far * 2, own, 2, features // 2)
    own_z, pair_z = recv[:, :, 0], recv[:, :, 1]
    even = jnp.where(p == 0, own_z, jnp.roll(pair_z, 1, axis=0))
    odd = jnp.where(p == 0, jnp.roll(pair_z, -1, axis=0), own_z)
    return jnp.stack([even, odd], axis=1).transpose(2, 0, 1, 3).reshape(own, width)


def solution(mesh):
    rows, cols = mesh.devices.shape
    side = 4
    shape = (rows // 4, 2, 2, side, cols // (2 * side), 2)
    fine = Mesh(mesh.devices.reshape(shape), LINE + PLANE + ("c",))
    row, col = LINE, PLANE + ("c",)
    in_specs = (
        P(row + col, None),
        P(col, None, row, None),
        P(col, None, row),
        P(),
        P(),
        P(),
    )
    out_specs = P(row + col, None)
    return jax.shard_map(local, mesh=fine, in_specs=in_specs, out_specs=out_specs, check_vma=False)
```

```python
import jax
import jax.numpy as jnp
from jax import lax
from jax.experimental import pallas as pl
from jax.experimental.pallas import tpu as pltpu
from jax.sharding import Mesh, PartitionSpec as P

SLOTS = 48
LINE = ("zh", "k", "p")
RING = ("zh", "k")
PLANE = ("x", "y")
PAIR = [(0, 1), (1, 0)]


def routing(expert_ids, gate_weights, capacity, expert):
    member = expert_ids == expert
    hits = jnp.sum(member.astype(jnp.int32), axis=2)
    rank = jnp.cumsum(hits, axis=1) - hits
    cap = lax.dynamic_index_in_dim(capacity, expert, 0, keepdims=False)
    weights = jnp.sum(jnp.where(member, gate_weights, 0.0), axis=2)
    offset = jnp.arange(hits.shape[0], dtype=jnp.int32)[:, None] * SLOTS
    return jnp.where((hits > 0) & (rank < cap), rank + offset, -1), weights


def start_total(total):
    @pl.when(pl.program_id(0) == 0)
    def _():
        total[...] = jnp.zeros_like(total)


def add_product(total, rows, tokens):
    total[...] += lax.dot_general(
        jnp.concatenate(rows, axis=0),
        tokens[...],
        (((1,), (1,)), ((), ())),
        preferred_element_type=jnp.float32,
    )


def unit_values(gate, up):
    return (gate / (1.0 + jnp.exp(-gate)) * up).astype(jnp.bfloat16)


def pick(hidden, hits):
    return jnp.dot(
        jnp.concatenate(hidden, axis=1), hits[...], preferred_element_type=jnp.float32
    )


def rest_kernel(gate_a, up_a, gate_b, up_b, tokens, hits, out, total):
    start_total(total)
    add_product(total, [gate_a[...], up_a[...], gate_b[...], up_b[...]], tokens)

    @pl.when(pl.program_id(0) == pl.num_programs(0) - 1)
    def _():
        n = gate_a.shape[0]
        hidden = [unit_values(total[i * n : (i + 1) * n], total[(i + 1) * n : (i + 2) * n]) for i in (0, 2)]
        picked = pick(hidden, hits)[n - out.shape[1] :].astype(out.dtype)
        for i in range(out.shape[0]):
            out[i] = picked


def main_kernel(own_a, pair_a, own_b, pair_b, tokens, hits, out, total):
    start_total(total)
    units = pair_a.shape[0] // 2
    kept = total.shape[0] // 4 - units
    rows = []
    for own, pair in ((own_a, pair_a), (own_b, pair_b)):
        rows += [own[:kept], own[units : units + kept], pair[...]]
    add_product(total, rows, tokens)

    @pl.when(pl.program_id(0) == pl.num_programs(0) - 1)
    def _():
        hidden = []
        for expert in range(2):
            base = expert * 2 * (kept + units)
            middle = base + 2 * kept
            near = unit_values(total[base : base + kept], total[base + kept : middle])
            far = unit_values(total[middle : middle + units], total[middle + units : middle + 2 * units])
            hidden.append(jnp.concatenate([far, near], axis=0))
        out[...] = pick(hidden, hits)[: out.shape[0]].astype(out.dtype)


def slotted_hidden(kernel, weights, tokens, hits, total_rows, out_shape):
    count, width = tokens.shape
    depth = width // 4
    whole = lambda shape: pl.BlockSpec(shape, lambda i: (0,) * len(shape))
    return pl.pallas_call(
        kernel,
        grid=(width // depth,),
        in_specs=[pl.BlockSpec((size, depth), lambda i, at=at: (at, i)) for _, size, at in weights]
        + [pl.BlockSpec((count, depth), lambda i: (0, i)), whole(hits.shape)],
        out_specs=whole(out_shape),
        scratch_shapes=[pltpu.VMEM((total_rows, count), jnp.float32)],
        out_shape=jax.ShapeDtypeStruct(out_shape, jnp.bfloat16),
        compiler_params=pltpu.CompilerParams(vmem_limit_bytes=60 * 2**20),
        cost_estimate=pl.CostEstimate(
            flops=2 * total_rows * width * count,
            bytes_accessed=2 * width * (total_rows + count),
            transcendentals=total_rows * count // 2,
        ),
    )(*[w for w, _, _ in weights], tokens, hits)


def output_kernel(p_ref, main, rest, own_a, pair_a, own_b, pair_b, combine, out, hidden):
    members, ends = rest.shape[0], rest.shape[1]
    both = main.shape[1] + ends
    units = both // 2
    for i in range(members):
        gathered = main[i].astype(jnp.float32)
        near = jnp.concatenate([gathered[units:], rest[i].astype(jnp.float32)], axis=0)
        own = pl.multiple_of(i * both + p_ref[0] * units, 32)
        other = pl.multiple_of(i * both + (1 - p_ref[0]) * units, 32)
        hidden[pl.ds(own, units), :] = near.astype(hidden.dtype)
        hidden[pl.ds(other, units), :] = gathered[:units].astype(hidden.dtype)
    cut = hidden.shape[1] // 2
    low, high = cut // 128 * 128, -(-cut // 128) * 128
    outputs = []
    for d_a, d_b in [(own_a, own_b), (pair_a, pair_b)]:
        of_a = jnp.dot(d_a[...], hidden[:, :high], preferred_element_type=jnp.float32)
        of_b = jnp.dot(d_b[...], hidden[:, low:], preferred_element_type=jnp.float32)
        pieces = [of_a[:, :low]]
        if high > low:
            middle = of_a[:, low:]
            is_a = lax.broadcasted_iota(jnp.int32, middle.shape, 1) < cut - low
            pieces.append(jnp.where(is_a, middle, of_b[:, : high - low]))
        pieces.append(of_b[:, high - low :])
        outputs.append(jnp.concatenate(pieces, axis=1).astype(jnp.bfloat16))
    outputs = jnp.concatenate(outputs, axis=0)
    out[...] = lax.dot_general(
        combine[...], outputs, (((1,), (1,)), ((), ())), preferred_element_type=jnp.float32
    ).astype(jnp.bfloat16)


def token_sums(p, main, rest, own_a, pair_a, own_b, pair_b, combine):
    features, units = own_a.shape
    count, slots = combine.shape
    return pl.pallas_call(
        output_kernel,
        in_specs=[pl.BlockSpec(memory_space=pltpu.SMEM)]
        + [pl.BlockSpec(memory_space=pltpu.VMEM)] * 7,
        out_specs=pl.BlockSpec(memory_space=pltpu.VMEM),
        scratch_shapes=[pltpu.VMEM((units, slots), jnp.bfloat16)],
        out_shape=jax.ShapeDtypeStruct((count, 2 * features), jnp.bfloat16),
        compiler_params=pltpu.CompilerParams(vmem_limit_bytes=40 * 2**20),
        cost_estimate=pl.CostEstimate(
            flops=8 * features * units * slots,
            bytes_accessed=8 * features * units,
            transcendentals=0,
        ),
    )(p.reshape(1), main, rest, own_a, pair_a, own_b, pair_b, combine)


def local(tokens, gate_up, down, expert_ids, gate_weights, capacity):
    core = lax.axis_index("c")
    k, p = lax.axis_index("k"), lax.axis_index("p")
    plane_index = lax.axis_index(PLANE)
    chips = lax.axis_size("x") * lax.axis_size("y")
    far = lax.axis_size("zh")
    own, width = tokens.shape
    group_rows = chips * 2 * own
    class_rows = far * group_rows
    class_slots = far * SLOTS

    def of_class(values, which):
        values = values.reshape((far, 2, 2) + values.shape[1:])
        return lax.dynamic_index_in_dim(
            lax.dynamic_index_in_dim(values, p, 2, keepdims=False), which, 1, keepdims=False
        )

    units = gate_up.shape[2]
    w_own = gate_up[0].reshape(2 * units, width)
    w_pair = lax.ppermute(w_own, "p", PAIR)

    chip_rows = lax.all_gather(tokens, RING + ("c",), axis=0, tiled=False)
    chip_rows = chip_rows.reshape(far, 2, 2, own, width)
    chip_rows = lax.dynamic_index_in_dim(chip_rows, core, 1, keepdims=False)
    chip_rows = chip_rows.reshape(2 * far * own, width)
    every = lax.all_gather(chip_rows, PLANE, axis=0, tiled=True)

    ids = of_class(expert_ids.reshape(far * 4, group_rows, -1), core)
    gates = of_class(gate_weights.reshape(far * 4, group_rows, -1), core)

    def by_row(values):
        values = values.reshape(far, chips, 2, own).transpose(1, 0, 2, 3)
        return values.reshape(class_rows)

    slot_index = jnp.arange(2 * class_slots, dtype=jnp.int32)
    hits, combine = [], []
    for e, expert in enumerate((plane_index * 2 + core, plane_index * 2 + 1 - core)):
        slots, weights = routing(ids, gates, capacity, expert)
        slots = by_row(jnp.where(slots >= 0, slots + e * class_slots, -1))
        hit = slots[:, None] == slot_index[None, :]
        hits.append(hit.astype(jnp.bfloat16))
        combine.append(jnp.where(hit, by_row(weights)[:, None], 0.0))
    hits = jnp.concatenate(hits, axis=0)
    combine = (combine[0] + combine[1]).astype(jnp.bfloat16)

    w_other = lax.ppermute(w_own, "c", PAIR)
    d_own = down[0].T
    d_other = lax.ppermute(d_own, "c", PAIR)
    line = far * 4
    swap = [(z, (z + 1) % line if z % 2 else (z - 1) % line) for z in range(line)]
    d_pair = lax.ppermute(d_own, LINE, swap)
    d_pair_other = lax.ppermute(d_pair, "c", PAIR)
    w_pair, w_other, d_other, d_pair_other, hits, combine = lax.optimization_barrier(
        (w_pair, w_other, d_other, d_pair_other, hits, combine)
    )
    w_pair_other = lax.ppermute(w_pair, "c", PAIR)

    ends = units // 4
    block = units // 3
    members = far * 2
    places = (units // block - 1, 2 * units // block - 1)
    rest = slotted_hidden(
        rest_kernel,
        [(w, block, at) for w in (w_own, w_other) for at in places],
        every,
        hits,
        4 * block,
        (members, ends, 2 * class_slots),
    )
    every, rest = lax.optimization_barrier((every, rest))
    rest = lax.all_to_all(rest, RING, split_axis=0, concat_axis=0, tiled=True)
    main = slotted_hidden(
        main_kernel,
        [(w, 2 * units, 0) for w in (w_own, w_pair, w_other, w_pair_other)],
        every,
        hits,
        4 * (2 * units - ends // 16 * 16),
        (2 * units - ends, 2 * class_slots),
    )
    main = lax.all_gather(main, RING, axis=0, tiled=False)
    summed = token_sums(p, main, rest, d_own, d_pair, d_other, d_pair_other, combine)

    arrived = lax.all_to_all(summed, PLANE, split_axis=0, concat_axis=0, tiled=True)
    arrived = arrived.reshape(chips, 2 * far * own, arrived.shape[1]).astype(jnp.float32)
    rows = jnp.sum(arrived, axis=0).astype(jnp.bfloat16)
    features = rows.shape[1]

    rows = rows.reshape(far, 2, own, features)[:, None]
    here = (jnp.arange(2) == core)[None, :, None, None, None]
    send = jnp.where(here, rows, jnp.zeros((), rows.dtype)).reshape(far * 4 * own, features)
    recv = lax.all_to_all(send, ("zh", "k", "c"), split_axis=0, concat_axis=0, tiled=True)
    recv = recv.reshape(far, 2, 2, own, features)
    recv = lax.dynamic_index_in_dim(recv, k, 2, keepdims=False)
    recv = recv.reshape(far * 2, own, 2, features // 2)
    own_z, pair_z = recv[:, :, 0], recv[:, :, 1]
    even = jnp.where(p == 0, own_z, jnp.roll(pair_z, 1, axis=0))
    odd = jnp.where(p == 0, jnp.roll(pair_z, -1, axis=0), own_z)
    return jnp.stack([even, odd], axis=1).transpose(2, 0, 1, 3).reshape(own, width)


def solution(mesh):
    rows, cols = mesh.devices.shape
    side = 4
    shape = (rows // 4, 2, 2, side, cols // (2 * side), 2)
    fine = Mesh(mesh.devices.reshape(shape), LINE + PLANE + ("c",))
    row, col = LINE, PLANE + ("c",)
    in_specs = (
        P(row + col, None),
        P(col, None, row, None),
        P(col, None, row),
        P(),
        P(),
        P(),
    )
    out_specs = P(row + col, None)
    return jax.shard_map(local, mesh=fine, in_specs=in_specs, out_specs=out_specs, check_vma=False)
```

```python
import jax
import jax.numpy as jnp
from jax import lax
from jax.experimental import pallas as pl
from jax.experimental.pallas import tpu as pltpu
from jax.sharding import Mesh, PartitionSpec as P

SLOTS = 48
LINE = ("zh", "k", "p")
RING = ("zh", "k")
PLANE = ("x", "y")
PAIR = [(0, 1), (1, 0)]


def routing(expert_ids, gate_weights, capacity, expert):
    member = expert_ids == expert
    hits = jnp.sum(member.astype(jnp.int32), axis=2)
    rank = jnp.cumsum(hits, axis=1) - hits
    cap = lax.dynamic_index_in_dim(capacity, expert, 0, keepdims=False)
    weights = jnp.sum(jnp.where(member, gate_weights, 0.0), axis=2)
    offset = jnp.arange(hits.shape[0], dtype=jnp.int32)[:, None] * SLOTS
    return jnp.where((hits > 0) & (rank < cap), rank + offset, -1), weights


def start_total(total):
    @pl.when(pl.program_id(0) == 0)
    def _():
        total[...] = jnp.zeros_like(total)


def add_product(total, rows, tokens):
    total[...] += lax.dot_general(
        jnp.concatenate(rows, axis=0),
        tokens[...],
        (((1,), (1,)), ((), ())),
        preferred_element_type=jnp.float32,
    )


def unit_values(gate, up):
    return (gate / (1.0 + jnp.exp(-gate)) * up).astype(jnp.bfloat16)


def pick(hidden, hits):
    return jnp.dot(
        jnp.concatenate(hidden, axis=1), hits[...], preferred_element_type=jnp.float32
    ).astype(jnp.bfloat16)


def rest_kernel(gate_a, up_a, gate_b, up_b, tokens, hits, out, total):
    start_total(total)
    add_product(total, [gate_a[...], up_a[...], gate_b[...], up_b[...]], tokens)

    @pl.when(pl.program_id(0) == pl.num_programs(0) - 1)
    def _():
        n = gate_a.shape[0]
        hidden = [unit_values(total[i * n : (i + 1) * n], total[(i + 1) * n : (i + 2) * n]) for i in (0, 2)]
        picked = pick(hidden, hits)
        for i in range(out.shape[0]):
            out[i] = picked


def main_kernel(own_a, pair_a, own_b, pair_b, tokens, hits, out, total):
    start_total(total)
    units = pair_a.shape[0] // 2
    kept = out.shape[0] - units
    rows = []
    for own, pair in ((own_a, pair_a), (own_b, pair_b)):
        rows += [own[:kept], own[units : units + kept], pair[...]]
    add_product(total, rows, tokens)

    @pl.when(pl.program_id(0) == pl.num_programs(0) - 1)
    def _():
        hidden = []
        for expert in range(2):
            base = expert * 2 * (kept + units)
            middle = base + 2 * kept
            near = unit_values(total[base : base + kept], total[base + kept : middle])
            far = unit_values(total[middle : middle + units], total[middle + units : middle + 2 * units])
            hidden.append(jnp.concatenate([near, far], axis=0))
        out[...] = pick(hidden, hits)


def slotted_hidden(kernel, weights, tokens, hits, total_rows, out_shape):
    count, width = tokens.shape
    depth = width // 4
    whole = lambda shape: pl.BlockSpec(shape, lambda i: (0,) * len(shape))
    return pl.pallas_call(
        kernel,
        grid=(width // depth,),
        in_specs=[pl.BlockSpec((size, depth), lambda i, at=at: (at, i)) for _, size, at in weights]
        + [pl.BlockSpec((count, depth), lambda i: (0, i)), whole(hits.shape)],
        out_specs=whole(out_shape),
        scratch_shapes=[pltpu.VMEM((total_rows, count), jnp.float32)],
        out_shape=jax.ShapeDtypeStruct(out_shape, jnp.bfloat16),
        compiler_params=pltpu.CompilerParams(vmem_limit_bytes=40 * 2**20),
        cost_estimate=pl.CostEstimate(
            flops=2 * total_rows * width * count,
            bytes_accessed=2 * width * (total_rows + count),
            transcendentals=total_rows * count // 2,
        ),
    )(*[w for w, _, _ in weights], tokens, hits)


def output_kernel(p_ref, main, rest, own_a, pair_a, own_b, pair_b, combine, out, hidden):
    members, ends = rest.shape[0], rest.shape[1]
    both = main.shape[1] + ends
    units = both // 2
    kept = units - ends
    for i in range(members):
        own = pl.multiple_of(i * both + p_ref[0] * units, ends)
        other = pl.multiple_of(i * both + (1 - p_ref[0]) * units, ends)
        hidden[pl.ds(own, kept), :] = main[i, :kept]
        hidden[pl.ds(own + kept, ends), :] = rest[i]
        hidden[pl.ds(other, units), :] = main[i, kept:]
    cut = hidden.shape[1] // 2
    low, high = cut // 128 * 128, -(-cut // 128) * 128
    outputs = []
    for d_a, d_b in [(own_a, own_b), (pair_a, pair_b)]:
        of_a = jnp.dot(d_a[...], hidden[:, :high], preferred_element_type=jnp.float32)
        of_b = jnp.dot(d_b[...], hidden[:, low:], preferred_element_type=jnp.float32)
        pieces = [of_a[:, :low]]
        if high > low:
            middle = of_a[:, low:]
            is_a = lax.broadcasted_iota(jnp.int32, middle.shape, 1) < cut - low
            pieces.append(jnp.where(is_a, middle, of_b[:, : high - low]))
        pieces.append(of_b[:, high - low :])
        outputs.append(jnp.concatenate(pieces, axis=1).astype(jnp.bfloat16))
    outputs = jnp.concatenate(outputs, axis=0)
    out[...] = lax.dot_general(
        combine[...], outputs, (((1,), (1,)), ((), ())), preferred_element_type=jnp.float32
    ).astype(jnp.bfloat16)


def token_sums(p, main, rest, own_a, pair_a, own_b, pair_b, combine):
    features, units = own_a.shape
    count, slots = combine.shape
    return pl.pallas_call(
        output_kernel,
        in_specs=[pl.BlockSpec(memory_space=pltpu.SMEM)]
        + [pl.BlockSpec(memory_space=pltpu.VMEM)] * 7,
        out_specs=pl.BlockSpec(memory_space=pltpu.VMEM),
        scratch_shapes=[pltpu.VMEM((units, slots), jnp.bfloat16)],
        out_shape=jax.ShapeDtypeStruct((count, 2 * features), jnp.bfloat16),
        compiler_params=pltpu.CompilerParams(vmem_limit_bytes=40 * 2**20),
        cost_estimate=pl.CostEstimate(
            flops=8 * features * units * slots,
            bytes_accessed=8 * features * units,
            transcendentals=0,
        ),
    )(p.reshape(1), main, rest, own_a, pair_a, own_b, pair_b, combine)


def local(tokens, gate_up, down, expert_ids, gate_weights, capacity):
    core = lax.axis_index("c")
    k, p = lax.axis_index("k"), lax.axis_index("p")
    plane_index = lax.axis_index(PLANE)
    chips = lax.axis_size("x") * lax.axis_size("y")
    far = lax.axis_size("zh")
    own, width = tokens.shape
    group_rows = chips * 2 * own
    class_rows = far * group_rows
    class_slots = far * SLOTS

    def of_class(values, which):
        values = values.reshape((far, 2, 2) + values.shape[1:])
        return lax.dynamic_index_in_dim(
            lax.dynamic_index_in_dim(values, p, 2, keepdims=False), which, 1, keepdims=False
        )

    units = gate_up.shape[2]
    w_own = gate_up[0].reshape(2 * units, width)
    w_pair = lax.ppermute(w_own, "p", PAIR)

    chip_rows = lax.all_gather(tokens, RING + ("c",), axis=0, tiled=False)
    chip_rows = chip_rows.reshape(far, 2, 2, own, width)
    chip_rows = lax.dynamic_index_in_dim(chip_rows, core, 1, keepdims=False)
    chip_rows = chip_rows.reshape(2 * far * own, width)
    every = lax.all_gather(chip_rows, PLANE, axis=0, tiled=True)

    ids = of_class(expert_ids.reshape(far * 4, group_rows, -1), core)
    gates = of_class(gate_weights.reshape(far * 4, group_rows, -1), core)

    def by_row(values):
        values = values.reshape(far, chips, 2, own).transpose(1, 0, 2, 3)
        return values.reshape(class_rows)

    slot_index = jnp.arange(2 * class_slots, dtype=jnp.int32)
    hits, combine = [], []
    for e, expert in enumerate((plane_index * 2 + core, plane_index * 2 + 1 - core)):
        slots, weights = routing(ids, gates, capacity, expert)
        slots = by_row(jnp.where(slots >= 0, slots + e * class_slots, -1))
        hit = slots[:, None] == slot_index[None, :]
        hits.append(hit.astype(jnp.bfloat16))
        combine.append(jnp.where(hit, by_row(weights)[:, None], 0.0))
    hits = jnp.concatenate(hits, axis=0)
    combine = (combine[0] + combine[1]).astype(jnp.bfloat16)

    w_other = lax.ppermute(w_own, "c", PAIR)
    d_own = down[0].T
    d_other = lax.ppermute(d_own, "c", PAIR)
    line = far * 4
    swap = [(z, (z + 1) % line if z % 2 else (z - 1) % line) for z in range(line)]
    d_pair = lax.ppermute(d_own, LINE, swap)
    d_pair_other = lax.ppermute(d_pair, "c", PAIR)
    w_pair, w_other, d_other, d_pair_other, hits, combine = lax.optimization_barrier(
        (w_pair, w_other, d_other, d_pair_other, hits, combine)
    )
    w_pair_other = lax.ppermute(w_pair, "c", PAIR)

    ends = units // 3
    kept = units - ends
    members = far * 2
    places = (kept // ends, (units + kept) // ends)
    rest = slotted_hidden(
        rest_kernel,
        [(w, ends, at) for w in (w_own, w_other) for at in places],
        every,
        hits,
        4 * ends,
        (members, ends, 2 * class_slots),
    )
    every, rest = lax.optimization_barrier((every, rest))
    rest = lax.all_to_all(rest, RING, split_axis=0, concat_axis=0, tiled=True)
    main = slotted_hidden(
        main_kernel,
        [(w, 2 * units, 0) for w in (w_own, w_pair, w_other, w_pair_other)],
        every,
        hits,
        4 * (units + kept),
        (units + kept, 2 * class_slots),
    )
    main = lax.all_gather(main, RING, axis=0, tiled=False)
    summed = token_sums(p, main, rest, d_own, d_pair, d_other, d_pair_other, combine)

    arrived = lax.all_to_all(summed, PLANE, split_axis=0, concat_axis=0, tiled=True)
    arrived = arrived.reshape(chips, 2 * far * own, arrived.shape[1]).astype(jnp.float32)
    rows = jnp.sum(arrived, axis=0).astype(jnp.bfloat16)
    features = rows.shape[1]

    rows = rows.reshape(far, 2, own, features)[:, None]
    here = (jnp.arange(2) == core)[None, :, None, None, None]
    send = jnp.where(here, rows, jnp.zeros((), rows.dtype)).reshape(far * 4 * own, features)
    recv = lax.all_to_all(send, ("zh", "k", "c"), split_axis=0, concat_axis=0, tiled=True)
    recv = recv.reshape(far, 2, 2, own, features)
    recv = lax.dynamic_index_in_dim(recv, k, 2, keepdims=False)
    recv = recv.reshape(far * 2, own, 2, features // 2)
    own_z, pair_z = recv[:, :, 0], recv[:, :, 1]
    even = jnp.where(p == 0, own_z, jnp.roll(pair_z, 1, axis=0))
    odd = jnp.where(p == 0, jnp.roll(pair_z, -1, axis=0), own_z)
    return jnp.stack([even, odd], axis=1).transpose(2, 0, 1, 3).reshape(own, width)


def solution(mesh):
    rows, cols = mesh.devices.shape
    side = 4
    shape = (rows // 4, 2, 2, side, cols // (2 * side), 2)
    fine = Mesh(mesh.devices.reshape(shape), LINE + PLANE + ("c",))
    row, col = LINE, PLANE + ("c",)
    in_specs = (
        P(row + col, None),
        P(col, None, row, None),
        P(col, None, row),
        P(),
        P(),
        P(),
    )
    out_specs = P(row + col, None)
    return jax.shard_map(local, mesh=fine, in_specs=in_specs, out_specs=out_specs, check_vma=False)
```
